32 devices in a mesh: grp: 4 (over x, core), blk: 8 (over z, y).
Axes of the slice: x: 2, y: 2, z: 4, core: 2. Of those that a mesh axis runs over, the one named last changes fastest.
Arguments:
- query: bfloat16 [8192, 512], P(('grp', 'blk')), may hold values from -6 to 6
- key: bfloat16 [8192, 512], P(('grp', 'blk')), may hold values from -6 to 6
- value: bfloat16 [8192, 512], P(('grp', 'blk')), may hold values from -6 to 6
- out_grad: bfloat16 [8192, 512], P(('grp', 'blk')), may hold values from -6 to 6
- partner: int32 [2, 8192], P(None, ('grp', 'blk')), may hold values from 0 to 127, as said below
- tiles: int32 [64, 6], P(('grp', 'blk')), may hold values from 0 to 15, as said below
- tile_count: int32 [64], P(('grp', 'blk')), may hold values from 1 to 6, as said below
Outputs:
- attended: bfloat16 [8192, 512], P(('grp', 'blk'))
- query_grad: bfloat16 [8192, 512], P(('grp', 'blk'))
- key_grad: bfloat16 [8192, 512], P(('grp', 'blk'))
- value_grad: bfloat16 [8192, 512], P(('grp', 'blk'))
The draws below stay inside these ranges and needn't reach their ends.
Inputs may be any that keep to these rules, and one draw needn't show every extreme that they name: `partner`: the matching of every round is symmetric: match[r, match[r, n]] = n for every node n. `tiles`: the entries of a row are distinct; the first entry of block k's row is k's own block within its cluster; block a lists block b among its first tile_count entries exactly when b lists a. `tile_count`: some block of every cluster uses all 6 slots.
All inputs are finite; a program needn't handle non-finite values.
Results may differ from the reference program's by a relative error of at most 0.014.
Values may be sent and summed in bfloat16 or wider, within the bound.
A program may use at most 64 MiB of HBM per device.

```python
import jax
import jax.numpy as jnp
from jax import lax

D = 512
HEADS = 8
HEAD_DIM = 64
NODE_DEV = 256
BLOCK = 128
TMAX = 6
ROUNDS = 2
CLUSTER = 2048
NODES = 8192


def paired_rows(key):
    base = jax.random.fold_in(key, 7)
    queries = jnp.clip(jax.random.normal(jax.random.fold_in(base, 1), (NODES, D), jnp.float32), -6.0, 6.0)
    keys = jnp.clip(jax.random.normal(jax.random.fold_in(base, 2), (NODES, D), jnp.float32), -6.0, 6.0)
    return (queries, keys)


def draw_query(key, part):
    return paired_rows(key)[0].astype(jnp.bfloat16)


def draw_key(key, part):
    return paired_rows(key)[1].astype(jnp.bfloat16)


def draw_partner(key, part):
    base = jax.random.fold_in(key, 21)
    units = NODES // NODE_DEV
    per_cluster = CLUSTER // NODE_DEV
    clusters = NODES // CLUSTER
    half = NODE_DEV // 2
    unit = jnp.arange(units, dtype=jnp.int32)
    owner = unit // per_cluster
    rank = unit % per_cluster

    def one_perm(subkey):
        return jax.random.permutation(subkey, half).astype(jnp.int32)
    table = []
    for step in range(ROUNDS):
        subkeys = jax.random.split(jax.random.fold_in(base, step), units)
        forward = jax.vmap(one_perm)(subkeys)
        inverse = jnp.argsort(forward, axis=1, stable=True).astype(jnp.int32)
        behind = (owner - step - 1) % clusters * per_cluster + rank
        second = inverse[behind]
        table.append(jnp.concatenate([forward, second], 1).reshape(NODES))
    return jnp.stack(table).astype(jnp.int32)


def block_links(key):
    base = jax.random.fold_in(key, 33)
    blocks = CLUSTER // BLOCK
    clusters = NODES // CLUSTER
    cycle = blocks - 1

    def one_cluster(subkey):
        first_key, second_key, third_key = jax.random.split(subkey, 3)
        rounds = jax.random.permutation(first_key, cycle)[:TMAX - 1].astype(jnp.int32)
        label = jax.random.permutation(second_key, blocks).astype(jnp.int32)
        place = jnp.argsort(label, stable=True).astype(jnp.int32)
        flips = jax.random.randint(third_key, (TMAX - 1, blocks), 0, 2).astype(jnp.int32)
        spot = place[None, :]
        turn = rounds[:, None]
        mate = jnp.where(spot == cycle, turn, jnp.where(spot == turn, cycle, (2 * turn - spot) % cycle))
        lower = jnp.minimum(spot, mate)
        keep = (jnp.take_along_axis(flips, lower, axis=1) == 1) | (spot == 0) | (mate == 0)
        entries = label[mate]
        candidates = jnp.concatenate([jnp.arange(blocks, dtype=jnp.int32)[None, :], entries], 0).T
        flags = jnp.concatenate([jnp.ones((1, blocks), jnp.int32), keep.astype(jnp.int32)], 0).T
        order = jnp.argsort(1 - flags, axis=1, stable=True)
        chosen = jnp.take_along_axis(candidates, order, axis=1)
        return (chosen.astype(jnp.int32), jnp.sum(flags, 1).astype(jnp.int32))
    subkeys = jax.random.split(base, clusters)
    chosen, counted = jax.vmap(one_cluster)(subkeys)
    return (chosen.reshape(clusters * blocks, TMAX).astype(jnp.int32), counted.reshape(clusters * blocks).astype(jnp.int32))


def draw_tiles(key, part):
    return block_links(key)[0]


def draw_tile_count(key, part):
    return block_links(key)[1]


def shard_levels(own_key, extent, cuts, low, high):
    loudness, own = 1.0, jax.random.fold_in(own_key, 6)
    for axis_at, parts in cuts:
        heights = jnp.exp(jax.random.uniform(jax.random.fold_in(own, axis_at), (parts,), jnp.float32, low / len(cuts), high / len(cuts)))
        loudness = loudness * jnp.repeat(heights, extent[axis_at] // parts).reshape([-1 if axis == axis_at else 1 for axis in range(len(extent))])
    return loudness


def scatter_about(key, dims, width, most, shards=(), kind=jnp.bfloat16):
    level = shard_levels(key, dims, shards, -0.22, 0.18) if shards else 1.0
    result = jax.random.normal(key, dims, jnp.float32) * width * level
    return jnp.minimum(jnp.maximum(result, -most), most).astype(kind)


def setup_inputs(seed: int = 0) -> dict:
    streams_of = jax.random.split(jax.random.key(seed), 8)
    query = draw_query(jax.random.fold_in(streams_of[7], 71), 0)
    key = draw_key(jax.random.fold_in(streams_of[7], 71), 0)
    value = scatter_about(streams_of[2], (NODES, D), 1.0, 6.0, ((0, 32),))
    out_grad = scatter_about(streams_of[3], (NODES, D), 1.0, 6.0, ((0, 32),))
    partner = draw_partner(jax.random.fold_in(streams_of[7], 71), 0)
    tiles = draw_tiles(jax.random.fold_in(streams_of[7], 71), 0)
    tile_count = draw_tile_count(jax.random.fold_in(streams_of[7], 71), 0)
    return dict(query=query, key=key, value=value, out_grad=out_grad, partner=partner, tiles=tiles, tile_count=tile_count)


NEG_BIG = -1.0e30


def settle(values):
    return lax.optimization_barrier(values.astype(jnp.bfloat16)).astype(jnp.float32)


def match_table(partner):
    per_cluster = CLUSTER // NODE_DEV
    clusters = NODES // CLUSTER
    half = NODE_DEV // 2
    node = jnp.arange(NODES, dtype=jnp.int32)
    unit = node // NODE_DEV
    owner = unit // per_cluster
    rank = unit % per_cluster
    first_half = (node % NODE_DEV) < half
    table = []
    for step in range(ROUNDS):
        ahead = ((owner + step + 1) % clusters) * per_cluster + rank
        behind = ((owner - step - 1) % clusters) * per_cluster + rank
        target = jnp.where(first_half, ahead * NODE_DEV + half + partner[step], behind * NODE_DEV + partner[step])
        table.append(target.astype(jnp.int32))
    return jnp.stack(table)


def cluster_pass(index, query, key, value, out_grad, match, tiles, tile_count):
    f32 = jnp.float32
    blocks = CLUSTER // BLOCK
    units = CLUSTER // NODE_DEV
    per_unit = NODE_DEV // BLOCK
    keys_tile = TMAX * BLOCK
    scale = HEAD_DIM ** -0.5
    first = index * CLUSTER

    def cluster_rows(array):
        return lax.dynamic_slice_in_dim(array, first, CLUSTER, 0)

    tile_ids = lax.dynamic_slice_in_dim(tiles, index * blocks, blocks, 0)
    tile_num = lax.dynamic_slice_in_dim(tile_count, index * blocks, blocks, 0)
    mates = lax.dynamic_slice_in_dim(match, first, CLUSTER, 1)
    shape = (blocks, BLOCK, HEADS, HEAD_DIM)
    q_f = cluster_rows(query).astype(f32).reshape(shape)
    g_f = cluster_rows(out_grad).astype(f32).reshape(shape)
    k_tile = cluster_rows(key).reshape(blocks, BLOCK, D)[tile_ids].astype(f32).reshape(blocks, keys_tile, HEADS, HEAD_DIM)
    v_tile = cluster_rows(value).reshape(blocks, BLOCK, D)[tile_ids].astype(f32).reshape(blocks, keys_tile, HEADS, HEAD_DIM)
    pair_shape = (ROUNDS, blocks, BLOCK, HEADS, HEAD_DIM)
    k_pair = key[mates].astype(f32).reshape(pair_shape)
    v_pair = value[mates].astype(f32).reshape(pair_shape)
    live = jnp.arange(TMAX, dtype=jnp.int32)[None, :] < tile_num[:, None]
    key_live = jnp.broadcast_to(live[:, :, None], (blocks, TMAX, BLOCK)).reshape(blocks, keys_tile)

    s_loc = jnp.einsum("bqhd,bkhd->bhqk", q_f, k_tile) * scale
    s_loc = jnp.where(key_live[:, None, None, :], s_loc, NEG_BIG)
    s_pair = jnp.einsum("bqhd,rbqhd->bhqr", q_f, k_pair) * scale
    top = jnp.maximum(jnp.max(s_loc, -1), jnp.max(s_pair, -1))
    e_loc = jnp.exp(s_loc - top[..., None])
    e_pair = jnp.exp(s_pair - top[..., None])
    total = jnp.sum(e_loc, -1) + jnp.sum(e_pair, -1)
    p_loc = e_loc / total[..., None]
    p_pair = e_pair / total[..., None]
    w_loc = settle(p_loc)
    w_pair = settle(p_pair)
    out_full = jnp.einsum("bhqk,bkhd->bqhd", w_loc, v_tile) + jnp.einsum("bhqr,rbqhd->bqhd", w_pair, v_pair)
    delta = jnp.transpose(jnp.sum(g_f * out_full, -1), (0, 2, 1))
    d_loc = jnp.einsum("bqhd,bkhd->bhqk", g_f, v_tile)
    d_pair = jnp.einsum("bqhd,rbqhd->bhqr", g_f, v_pair)
    z_loc = settle(p_loc * (d_loc - delta[..., None]))
    z_pair = settle(p_pair * (d_pair - delta[..., None]))
    q_grad = (jnp.einsum("bhqk,bkhd->bqhd", z_loc, k_tile) + jnp.einsum("bhqr,rbqhd->bqhd", z_pair, k_pair)) * scale
    c_key = (jnp.einsum("bhqk,bqhd->bkhd", z_loc, q_f) * scale).reshape(units, per_unit, TMAX, BLOCK, D)
    c_val = jnp.einsum("bhqk,bqhd->bkhd", w_loc, g_f).reshape(units, per_unit, TMAX, BLOCK, D)
    unit_ids = tile_ids.reshape(units, per_unit, TMAX)

    def spread_unit(ids_one, values_one):
        return jnp.zeros((blocks, BLOCK, D), f32).at[ids_one].add(values_one)

    part_key = jnp.sum(settle(jax.vmap(spread_unit)(unit_ids, c_key)), 0).reshape(CLUSTER, D)
    part_val = jnp.sum(settle(jax.vmap(spread_unit)(unit_ids, c_val)), 0).reshape(CLUSTER, D)
    term_key = (jnp.einsum("bhqr,bqhd->rbqhd", z_pair, q_f) * scale).astype(jnp.bfloat16).reshape(ROUNDS, CLUSTER, D)
    term_val = jnp.einsum("bhqr,bqhd->rbqhd", w_pair, g_f).astype(jnp.bfloat16).reshape(ROUNDS, CLUSTER, D)
    attended = out_full.reshape(CLUSTER, D).astype(jnp.bfloat16)
    query_grad = q_grad.reshape(CLUSTER, D).astype(jnp.bfloat16)
    return attended, query_grad, part_key, part_val, term_key, term_val


def reference(query, key, value, out_grad, partner, tiles, tile_count):
    match = match_table(partner)
    clusters = NODES // CLUSTER

    def run_cluster(index):
        return cluster_pass(index, query, key, value, out_grad, match, tiles, tile_count)

    attended, query_grad, part_key, part_val, term_key, term_val = lax.map(run_cluster, jnp.arange(clusters, dtype=jnp.int32))
    attended = attended.reshape(NODES, D)
    query_grad = query_grad.reshape(NODES, D)
    term_key = jnp.moveaxis(term_key, 1, 0).reshape(ROUNDS, NODES, D)
    term_val = jnp.moveaxis(term_val, 1, 0).reshape(ROUNDS, NODES, D)
    back_key = part_key.reshape(NODES, D)
    back_val = part_val.reshape(NODES, D)
    for step in range(ROUNDS):
        back_key = back_key + term_key[step][match[step]].astype(jnp.float32)
        back_val = back_val + term_val[step][match[step]].astype(jnp.float32)
    return attended, query_grad, back_key.astype(jnp.bfloat16), back_val.astype(jnp.bfloat16)
```

```python
import functools

import jax
import jax.numpy as jnp
from jax import lax
from jax.experimental import pallas as pl
from jax.experimental.pallas import tpu as pltpu
from jax.sharding import PartitionSpec as P

HEADS = 8
HEAD_DIM = 64
BLOCK = 128
TMAX = 6
ROUNDS = 2
NEG_BIG = -1e30
SCALE = HEAD_DIM**-0.5
MESH = pl.DeviceIdType.MESH
VMEM = pltpu.VMEM
F32 = jnp.float32
BF16 = jnp.bfloat16
LIMIT = 40 * 1024 * 1024


def grp_offsets(clusters):
    found = set()
    for step in range(ROUNDS):
        found.add((step + 1) % clusters)
        found.add((-step - 1) % clusters)
    return sorted(found - {0})


def greet(clusters, team, row, me):
    barrier = pltpu.get_barrier_semaphore()
    offsets = grp_offsets(clusters)
    for offset in offsets:
        pl.semaphore_signal(
            barrier,
            inc=1,
            device_id=(lax.rem(row + offset, clusters), me),
            device_id_type=MESH,
        )
    for offset in range(1, team):
        pl.semaphore_signal(
            barrier, inc=1, device_id=(row, lax.rem(me + offset, team)), device_id_type=MESH
        )
    return barrier, len(offsets) + team - 1


def remote(src, dst, send_sem, recv_sem, target):
    return pltpu.make_async_remote_copy(
        src_ref=src,
        dst_ref=dst,
        send_sem=send_sem,
        recv_sem=recv_sem,
        device_id=target,
        device_id_type=MESH,
    )


def head_marks(rows, slot, width):
    at = lax.broadcasted_iota(jnp.int32, (rows, width), 0)
    column = lax.broadcasted_iota(jnp.int32, (rows, width), 1)
    hit = at == (column // HEAD_DIM) * 8 + slot
    return jnp.where(hit, 1.0, 0.0).astype(BF16)


def pick_rows(slots):
    at = lax.broadcasted_iota(jnp.int32, (BLOCK, BLOCK), 0)
    hit = jnp.where(at == jnp.broadcast_to(slots, (BLOCK, BLOCK)), 1.0, 0.0)
    return hit.T.astype(BF16)


def dot_last(left, right):
    return lax.dot_general(left, right, (((1,), (1,)), ((), ())), preferred_element_type=F32)


def dot(left, right):
    return jnp.dot(left, right, preferred_element_type=F32)


def spread_kernel(
    clusters,
    team,
    q_ref,
    k_ref,
    v_ref,
    g_ref,
    partner_ref,
    meta_ref,
    x_ref,
    pair_ref,
    meta_all_ref,
    kp_ref,
    vp_ref,
    packed,
    pair_out,
    kbuf,
    vbuf,
    x_send,
    x_recv,
    p_send,
    p_recv,
    m_send,
    m_recv,
    g_send,
    g_recv,
):
    row = lax.axis_index("grp")
    me = lax.axis_index("blk")
    width = q_ref.shape[1]
    barrier, count = greet(clusters, team, row, me)

    for head in range(team):
        left = head * HEAD_DIM
        for half in range(2):
            rows = slice(half * BLOCK, (half + 1) * BLOCK)
            cols = slice(left, left + HEAD_DIM)
            packed[head, half] = jnp.concatenate([q_ref[rows, cols], g_ref[rows, cols]], 1)
            packed[head, 2 + half] = jnp.concatenate([k_ref[rows, cols], v_ref[rows, cols]], 1)

    pl.semaphore_wait(barrier, count)

    moves = []
    for step in range(ROUNDS):
        by = step + 1
        ahead = (lax.rem(row + by, clusters), me)
        behind = (lax.rem(row + clusters - by, clusters), me)
        for at, (src, dst) in enumerate(((k_ref, kbuf), (v_ref, vbuf))):
            for half, target in ((0, behind), (1, ahead)):
                rows = pl.ds((1 - half) * BLOCK, BLOCK)
                index = (step * 2 + at) * 2 + half
                copy = remote(
                    src.at[rows], dst.at[step, half], g_send.at[index], g_recv.at[index], target
                )
                copy.start()
                moves.append(copy)

    sends = []
    for offset in range(1, team):
        peer = lax.rem(me + offset, team)
        target = (row, peer)
        copy = remote(
            meta_ref, meta_all_ref.at[me], m_send.at[offset], m_recv.at[offset], target
        )
        copy.start()
        sends.append(copy)
    for offset in range(1, team):
        peer = lax.rem(me + offset, team)
        target = (row, peer)
        copy = remote(packed.at[peer], x_ref.at[me], x_send.at[offset], x_recv.at[offset], target)
        copy.start()
        sends.append(copy)
    x_ref[me] = packed[me]
    meta_all_ref[me] = meta_ref[...]

    for copy in moves:
        copy.wait()
    marks = [head_marks(8 * HEADS, slot, width) for slot in range(2 * ROUNDS)]
    for half in range(2):
        rows = slice(half * BLOCK, (half + 1) * BLOCK)
        total = None
        for step in range(ROUNDS):
            pick = pick_rows(partner_ref[step : step + 1, rows])
            for at, (buf, out, near) in enumerate(
                ((kbuf, kp_ref, q_ref), (vbuf, vp_ref, g_ref))
            ):
                taken = dot(pick, buf[step, half])
                out[step, rows] = taken.astype(BF16)
                product = near[rows].astype(F32) * taken
                high = product.astype(BF16)
                low = (product - high.astype(F32)).astype(BF16)
                mark = marks[at * ROUNDS + step]
                part = dot_last(mark, high) + dot_last(mark, low)
                total = part if total is None else total + part
        pair_out[:, half] = total.reshape(HEADS, 8, BLOCK)
    for offset in range(1, team):
        peer = lax.rem(me + offset, team)
        copy = remote(
            pair_out.at[peer], pair_ref.at[me], p_send.at[offset], p_recv.at[offset], (row, peer)
        )
        copy.start()
        sends.append(copy)
    pair_ref[me] = pair_out[me]
    for copy in sends:
        copy.wait()


def attend_kernel(x_ref, pair_ref, meta_ref, y_ref, pw_ref, kvt, acc):
    team = x_ref.shape[0]
    blocks = 2 * team
    lane = lax.broadcasted_iota(jnp.int32, (BLOCK, BLOCK), 1) < HEAD_DIM
    for unit in range(team):
        for half in range(2):
            kvt[2 * unit + half] = x_ref[unit, 2 + half].astype(F32).T.astype(BF16)
    acc[...] = jnp.zeros_like(acc)

    def body(block, carry):
        unit = block // 2
        half = block % 2
        qg = x_ref[unit, half].astype(F32)
        qg2 = jnp.concatenate([jnp.where(lane, qg, 0.0), jnp.where(lane, 0.0, qg)], 0).astype(BF16)
        ids = [meta_ref[unit, half, slot] for slot in range(TMAX)]
        live = meta_ref[unit, half, TMAX]
        pair = pair_ref[unit, half]
        s_pair = [pair[r : r + 1] * SCALE for r in range(ROUNDS)]
        d_pair = [pair[ROUNDS + r : ROUNDS + r + 1] for r in range(ROUNDS)]
        s_loc, d_loc = [], []
        top = functools.reduce(jnp.maximum, s_pair)
        for slot in range(TMAX):
            kv = x_ref[ids[slot] // 2, 2 + ids[slot] % 2]
            both = dot_last(kv, qg2)
            scores = both[:, :BLOCK] * SCALE + jnp.where(slot < live, 0.0, NEG_BIG)
            s_loc.append(scores)
            d_loc.append(both[:, BLOCK:])
            top = jnp.maximum(top, jnp.max(scores, 0, keepdims=True))
        e_pair = [jnp.exp(s - top) for s in s_pair]
        total = functools.reduce(jnp.add, e_pair)
        e_loc = []
        for slot in range(TMAX):
            e = jnp.exp(s_loc[slot] - top)
            e_loc.append(e)
            total = total + jnp.sum(e, 0, keepdims=True)
        inverse = 1.0 / total
        p_pair = [e * inverse for e in e_pair]
        w_pair = [p.astype(BF16).astype(F32) for p in p_pair]
        delta = functools.reduce(jnp.add, [w * d for w, d in zip(w_pair, d_pair)])
        p_loc, w_loc = [], []
        for slot in range(TMAX):
            p = e_loc[slot] * inverse
            w = p.astype(BF16)
            p_loc.append(p)
            w_loc.append(w)
            delta = delta + jnp.sum(w.astype(F32) * d_loc[slot], 0, keepdims=True)
        z_pair = [(p * (d - delta)).astype(BF16).astype(F32) for p, d in zip(p_pair, d_pair)]
        pw_ref[unit, half] = jnp.concatenate(
            w_pair + z_pair + [jnp.zeros((8 - 2 * ROUNDS, BLOCK), F32)], 0
        )
        back = None
        for slot in range(TMAX):
            z = (p_loc[slot] * (d_loc[slot] - delta)).astype(BF16)
            zw = jnp.concatenate([z, w_loc[slot]], 1)
            acc[ids[slot]] += dot(zw, qg2)
            part = dot(kvt[ids[slot]], zw)
            back = part if back is None else back + part
        turned = jnp.concatenate([back[:HEAD_DIM, :BLOCK] * SCALE, back[HEAD_DIM:, BLOCK:]], 0)
        y_ref[unit, half] = turned.T.astype(BF16)
        return carry

    lax.fori_loop(0, blocks, body, 0, unroll=2)
    for unit in range(team):
        for half in range(2):
            grads = acc[2 * unit + half]
            y_ref[unit, 2 + half] = jnp.where(lane, grads * SCALE, grads).astype(BF16)


def collect_kernel(
    clusters,
    team,
    y_ref,
    pw_ref,
    q_ref,
    g_ref,
    kp_ref,
    vp_ref,
    partner_ref,
    out_ref,
    dq_ref,
    dk_ref,
    dv_ref,
    ybuf,
    pbuf,
    terms,
    tbuf,
    y_send,
    y_recv,
    p_send,
    p_recv,
    g_send,
    g_recv,
):
    row = lax.axis_index("grp")
    me = lax.axis_index("blk")
    width = q_ref.shape[1]
    barrier, count = greet(clusters, team, row, me)
    pl.semaphore_wait(barrier, count)
    small, large = [], []
    for offset in range(1, team):
        peer = lax.rem(me + offset, team)
        copy = remote(
            pw_ref.at[peer], pbuf.at[me], p_send.at[offset], p_recv.at[offset], (row, peer)
        )
        copy.start()
        small.append(copy)
    for offset in range(1, team):
        peer = lax.rem(me + offset, team)
        copy = remote(
            y_ref.at[peer], ybuf.at[me], y_send.at[offset], y_recv.at[offset], (row, peer)
        )
        copy.start()
        large.append(copy)
    pbuf[me] = pw_ref[me]
    ybuf[me] = y_ref[me]
    for copy in small:
        copy.wait()

    marks = [head_marks(BLOCK, slot, width) for slot in range(2 * ROUNDS)]
    moves = []
    for half in range(2):
        rows = slice(half * BLOCK, (half + 1) * BLOCK)
        flat = pbuf[:, half].reshape(8 * HEADS, BLOCK)
        flat = jnp.concatenate([flat, jnp.zeros((BLOCK - 8 * HEADS, BLOCK), F32)], 0)
        turned = flat.T.astype(BF16)
        out_add = None
        dq_add = None
        for step in range(ROUNDS):
            by = step + 1
            w = dot(turned, marks[step])
            z = dot(turned, marks[ROUNDS + step]) * SCALE
            terms[step, half, :, :width] = (z * q_ref[rows].astype(F32)).astype(BF16)
            terms[step, half, :, width:] = (w * g_ref[rows].astype(F32)).astype(BF16)
            shift = by if half == 0 else clusters - by
            target = (lax.rem(row + shift, clusters), me)
            index = step * 2 + half
            copy = remote(
                terms.at[step, half],
                tbuf.at[step, 1 - half],
                g_send.at[index],
                g_recv.at[index],
                target,
            )
            copy.start()
            moves.append(copy)
            out_part = w * vp_ref[step, rows].astype(F32)
            dq_part = z * kp_ref[step, rows].astype(F32)
            out_add = out_part if out_add is None else out_add + out_part
            dq_add = dq_part if dq_add is None else dq_add + dq_part
        out_hold = out_add
        dq_hold = dq_add
        dv_ref[rows] = out_hold.astype(BF16)
        dk_ref[rows] = dq_hold.astype(BF16)

    for copy in large:
        copy.wait()

    def heads_of(half, left):
        parts = [ybuf[head, half][:, left : left + HEAD_DIM] for head in range(team)]
        return jnp.concatenate(parts, 1).astype(F32)

    for half in range(2):
        rows = slice(half * BLOCK, (half + 1) * BLOCK)
        dq_ref[rows] = (heads_of(half, 0) + dk_ref[rows].astype(F32)).astype(BF16)
        out_ref[rows] = (heads_of(half, HEAD_DIM) + dv_ref[rows].astype(F32)).astype(BF16)

    for copy in moves:
        copy.wait()
    for half in range(2):
        rows = slice(half * BLOCK, (half + 1) * BLOCK)
        back = None
        for step in range(ROUNDS):
            pick = pick_rows(partner_ref[step : step + 1, rows])
            part = dot(pick, tbuf[step, half])
            back = part if back is None else back + part
        dk_ref[rows] = (heads_of(2 + half, 0) + back[:, :width]).astype(BF16)
        dv_ref[rows] = (heads_of(2 + half, HEAD_DIM) + back[:, width:]).astype(BF16)


def shards(clusters, team, query, key, value, out_grad, partner, tiles, tile_count):
    nodes, width = query.shape
    meta = jnp.concatenate([tiles, tile_count[:, None]], 1)
    meta = jnp.pad(meta, ((0, 8 - meta.shape[0]), (0, 128 - meta.shape[1])))
    shape = jax.ShapeDtypeStruct
    whole = pl.BlockSpec(memory_space=VMEM)
    dma = pltpu.SemaphoreType.DMA
    big = (team, 4, BLOCK, BLOCK)
    few = (team, 2, 8, BLOCK)
    x, pair, meta_all, kp, vp = pl.pallas_call(
        functools.partial(spread_kernel, clusters, team),
        out_shape=(
            shape(big, BF16),
            shape(few, F32),
            shape((team, 8, 128), jnp.int32),
            shape((ROUNDS, nodes, width), BF16),
            shape((ROUNDS, nodes, width), BF16),
        ),
        in_specs=[whole] * 6,
        out_specs=(whole,) * 5,
        scratch_shapes=[
            VMEM(big, BF16),
            VMEM(few, F32),
            VMEM((ROUNDS, 2, BLOCK, width), BF16),
            VMEM((ROUNDS, 2, BLOCK, width), BF16),
        ]
        + [dma((team,))] * 6
        + [dma((4 * ROUNDS,))] * 2,
        compiler_params=pltpu.CompilerParams(
            collective_id=0, has_side_effects=True, vmem_limit_bytes=LIMIT
        ),
    )(query, key, value, out_grad, partner, meta)
    y, pw = pl.pallas_call(
        attend_kernel,
        out_shape=(shape(big, BF16), shape(few, F32)),
        in_specs=[whole, whole, pl.BlockSpec(memory_space=pltpu.SMEM)],
        out_specs=(whole, whole),
        scratch_shapes=[
            VMEM((2 * team, BLOCK, BLOCK), BF16),
            VMEM((2 * team, BLOCK, BLOCK), F32),
        ],
        compiler_params=pltpu.CompilerParams(vmem_limit_bytes=LIMIT),
    )(x, pair, meta_all)
    return pl.pallas_call(
        functools.partial(collect_kernel, clusters, team),
        out_shape=(shape((nodes, width), BF16),) * 4,
        in_specs=[whole] * 7,
        out_specs=(whole,) * 4,
        scratch_shapes=[
            VMEM(big, BF16),
            VMEM(few, F32),
            VMEM((ROUNDS, 2, BLOCK, 2 * width), BF16),
            VMEM((ROUNDS, 2, BLOCK, 2 * width), BF16),
        ]
        + [dma((team,))] * 4
        + [dma((2 * ROUNDS,))] * 2,
        compiler_params=pltpu.CompilerParams(
            collective_id=1, has_side_effects=True, vmem_limit_bytes=LIMIT
        ),
    )(y, pw, query, out_grad, kp, vp, partner)


def solution(mesh):
    rows = P(("grp", "blk"), None)
    in_specs = (rows, rows, rows, rows, P(None, ("grp", "blk")), rows, P(("grp", "blk")))
    return jax.shard_map(
        functools.partial(shards, mesh.shape["grp"], mesh.shape["blk"]),
        mesh=mesh,
        in_specs=in_specs,
        out_specs=(rows,) * 4,
        check_vma=False,
    )
```

```python
import functools

import jax
import jax.numpy as jnp
from jax import lax
from jax.experimental import pallas as pl
from jax.experimental.pallas import tpu as pltpu
from jax.sharding import PartitionSpec as P

HEADS = 8
HEAD_DIM = 64
BLOCK = 128
TMAX = 6
ROUNDS = 2
NEG_BIG = -1e30
SCALE = HEAD_DIM**-0.5
MESH = pl.DeviceIdType.MESH
VMEM = pltpu.VMEM
F32 = jnp.float32
BF16 = jnp.bfloat16
LIMIT = 56 * 1024 * 1024


def grp_offsets(clusters):
    found = set()
    for step in range(ROUNDS):
        found.add((step + 1) % clusters)
        found.add((-step - 1) % clusters)
    return sorted(found - {0})


def greet(clusters, team, row, me):
    barrier = pltpu.get_barrier_semaphore()
    offsets = grp_offsets(clusters)
    for offset in offsets:
        pl.semaphore_signal(
            barrier,
            inc=1,
            device_id=(lax.rem(row + offset, clusters), me),
            device_id_type=MESH,
        )
    for offset in range(1, team):
        pl.semaphore_signal(
            barrier, inc=1, device_id=(row, lax.rem(me + offset, team)), device_id_type=MESH
        )
    return barrier, len(offsets) + team - 1


def remote(src, dst, send_sem, recv_sem, target):
    return pltpu.make_async_remote_copy(
        src_ref=src,
        dst_ref=dst,
        send_sem=send_sem,
        recv_sem=recv_sem,
        device_id=target,
        device_id_type=MESH,
    )


def head_marks(rows, slot, width):
    at = lax.broadcasted_iota(jnp.int32, (rows, width), 0)
    column = lax.broadcasted_iota(jnp.int32, (rows, width), 1)
    hit = at == (column // HEAD_DIM) * 8 + slot
    return jnp.where(hit, 1.0, 0.0).astype(BF16)


def pick_rows(slots):
    at = lax.broadcasted_iota(jnp.int32, (BLOCK, BLOCK), 0)
    hit = jnp.where(at == jnp.broadcast_to(slots, (BLOCK, BLOCK)), 1.0, 0.0)
    return hit.T.astype(BF16)


def dot_last(left, right):
    return lax.dot_general(left, right, (((1,), (1,)), ((), ())), preferred_element_type=F32)


def dot(left, right):
    return jnp.dot(left, right, preferred_element_type=F32)


def fused_kernel(
    clusters,
    team,
    q_hbm,
    k_hbm,
    v_hbm,
    g_hbm,
    partner_ref,
    meta_ref,
    out_ref,
    dq_ref,
    dk_ref,
    dv_ref,
    near,
    far,
    qg_out,
    kv_out,
    qg_in,
    kv_in,
    pair_out,
    pair_in,
    meta_in,
    meta_s,
    picked,
    qg2,
    kvt,
    zw_all,
    oq_out,
    oq_in,
    dkv_out,
    dkv_in,
    pw_out,
    pw_in,
    pw_far,
    load_sem,
    meta_sem,
    qg_send,
    qg_recv,
    kv_send,
    kv_recv,
    m_send,
    m_recv,
    p_send,
    p_recv,
    o_send,
    o_recv,
    d_send,
    d_recv,
    w_send,
    w_recv,
    g_send,
    g_recv,
    f_send,
    f_recv,
):
    row = lax.axis_index("grp")
    me = lax.axis_index("blk")
    width = q_hbm.shape[1]
    blocks = 2 * team
    barrier, count = greet(clusters, team, row, me)
    q_at, k_at, v_at, g_at = range(4)

    loads = [
        pltpu.make_async_copy(src, near.at[at], load_sem.at[at])
        for at, src in enumerate((q_hbm, k_hbm, v_hbm, g_hbm))
    ]
    for load in loads:
        load.start()
    for load in loads:
        load.wait()

    def after(offset):
        return lax.rem(me + offset, team)

    def before(offset):
        return lax.rem(me + team - offset, team)

    def pack(out, one, two):
        for head in range(team):
            cols = slice(head * HEAD_DIM, (head + 1) * HEAD_DIM)
            for half in range(2):
                rows = slice(half * BLOCK, (half + 1) * BLOCK)
                out[head, half] = jnp.concatenate([near[one, rows, cols], near[two, rows, cols]], 1)

    pack(kv_out, k_at, v_at)
    pl.semaphore_wait(barrier, count)

    def across(out, into, send, recv, offset):
        peer = after(offset)
        return remote(out.at[peer], into.at[me], send.at[offset], recv.at[offset], (row, peer))

    def back_to(out, into, send, recv, offset):
        peer = before(offset)
        return remote(out.at[peer], into.at[me], send.at[offset], recv.at[offset], (row, peer))

    def matched(at, step, half):
        by = step + 1
        shift = by if half == 1 else clusters - by
        index = (at * ROUNDS + step) * 2 + half
        rows = pl.ds((1 - half) * BLOCK, BLOCK)
        return remote(
            near.at[at, rows],
            far.at[at, step, half],
            g_send.at[index],
            g_recv.at[index],
            (lax.rem(row + shift, clusters), me),
        )

    def meta_move(offset):
        peer = after(offset)
        return remote(
            meta_ref, meta_in.at[me], m_send.at[offset], m_recv.at[offset], (row, peer)
        )

    def all_matched(kinds):
        return [matched(at, step, half) for at in kinds for step in range(ROUNDS) for half in range(2)]

    metas = [meta_move(offset) for offset in range(1, team)]
    kv_moves = [across(kv_out, kv_in, kv_send, kv_recv, offset) for offset in range(1, team)]
    qg_moves = [across(qg_out, qg_in, qg_send, qg_recv, offset) for offset in range(1, team)]
    first = all_matched((k_at, v_at))
    second = all_matched((q_at, g_at))
    for copy in metas + first + kv_moves:
        copy.start()
    pack(qg_out, q_at, g_at)
    for copy in qg_moves + second:
        copy.start()
    kv_in[me] = kv_out[me]
    qg_in[me] = qg_out[me]
    meta_in[me] = meta_ref[...]
    zw_all[blocks * TMAX] = jnp.zeros((BLOCK, 2 * BLOCK), BF16)
    for copy in metas:
        copy.wait()
    to_scalar = pltpu.make_async_copy(meta_in, meta_s, meta_sem)
    to_scalar.start()
    to_scalar.wait()
    for copy in kv_moves:
        copy.wait()

    def turn(unit, carry):
        for half in range(2):
            kvt[2 * unit + half] = kv_in[unit, half].astype(F32).T.astype(BF16)
        return carry

    lax.fori_loop(0, team, turn, 0)

    for copy in first:
        copy.wait()
    marks = [head_marks(8 * HEADS, slot, width) for slot in range(2 * ROUNDS)]
    for half in range(2):
        rows = slice(half * BLOCK, (half + 1) * BLOCK)
        total = None
        for step in range(ROUNDS):
            pick = pick_rows(partner_ref[step : step + 1, rows])
            for at, (kind, own) in enumerate(((k_at, q_at), (v_at, g_at))):
                taken = dot(pick, far[kind, step, half])
                picked[at, step, rows] = taken.astype(BF16)
                product = near[own, rows].astype(F32) * taken
                high = product.astype(BF16)
                low = (product - high.astype(F32)).astype(BF16)
                mark = marks[at * ROUNDS + step]
                part = dot_last(mark, high) + dot_last(mark, low)
                total = part if total is None else total + part
        pair_out[:, half] = total.reshape(HEADS, 8, BLOCK)
    pairs = [across(pair_out, pair_in, p_send, p_recv, offset) for offset in range(1, team)]
    for copy in pairs:
        copy.start()
    pair_in[me] = pair_out[me]

    lane = lax.broadcasted_iota(jnp.int32, (BLOCK, BLOCK), 1) < HEAD_DIM

    def attend(unit, half):
        block = 2 * unit + half
        qg = qg_in[unit, half].astype(F32)
        split = jnp.concatenate([jnp.where(lane, qg, 0.0), jnp.where(lane, 0.0, qg)], 0)
        split = split.astype(BF16)
        qg2[block] = split
        ids = [meta_s[unit, half, slot] for slot in range(TMAX)]
        live = meta_s[unit, half, TMAX]
        pair = pair_in[unit, half]
        s_pair = [pair[r : r + 1] * SCALE for r in range(ROUNDS)]
        d_pair = [pair[ROUNDS + r : ROUNDS + r + 1] for r in range(ROUNDS)]
        s_loc, d_loc = [], []
        top = functools.reduce(jnp.maximum, s_pair)
        for slot in range(TMAX):
            kv = kv_in[ids[slot] // 2, ids[slot] % 2]
            both = dot_last(kv, split)
            scores = both[:, :BLOCK] * SCALE + jnp.where(slot < live, 0.0, NEG_BIG)
            s_loc.append(scores)
            d_loc.append(both[:, BLOCK:])
            top = jnp.maximum(top, jnp.max(scores, 0, keepdims=True))
        e_pair = [jnp.exp(s - top) for s in s_pair]
        total = functools.reduce(jnp.add, e_pair)
        e_loc = []
        for slot in range(TMAX):
            e = jnp.exp(s_loc[slot] - top)
            e_loc.append(e)
            total = total + jnp.sum(e, 0, keepdims=True)
        inverse = 1.0 / total
        p_pair = [e * inverse for e in e_pair]
        w_pair = [p.astype(BF16).astype(F32) for p in p_pair]
        delta = functools.reduce(jnp.add, [w * d for w, d in zip(w_pair, d_pair)])
        p_loc, w_loc = [], []
        for slot in range(TMAX):
            p = e_loc[slot] * inverse
            w = p.astype(BF16)
            p_loc.append(p)
            w_loc.append(w)
            delta = delta + jnp.sum(w.astype(F32) * d_loc[slot], 0, keepdims=True)
        z_pair = [(p * (d - delta)).astype(BF16).astype(F32) for p, d in zip(p_pair, d_pair)]
        pw_out[unit, half] = jnp.concatenate(
            w_pair + z_pair + [jnp.zeros((8 - 2 * ROUNDS, BLOCK), F32)], 0
        )
        back = None
        for slot in range(TMAX):
            z = (p_loc[slot] * (d_loc[slot] - delta)).astype(BF16)
            zw = jnp.concatenate([z, w_loc[slot]], 1)
            zw_all[block * TMAX + slot] = zw
            part = dot(kvt[ids[slot]], zw)
            back = part if back is None else back + part
        turned = jnp.concatenate([back[:HEAD_DIM, :BLOCK] * SCALE, back[HEAD_DIM:, BLOCK:]], 0)
        oq_out[unit, half] = turned.T.astype(BF16)

    def attend_unit(offset, carry):
        unit = before(offset)

        @pl.when(offset > 0)
        def _():
            across(qg_out, qg_in, qg_send, qg_recv, offset).wait()
            across(pair_out, pair_in, p_send, p_recv, offset).wait()

        for half in range(2):
            attend(unit, half)

        @pl.when(offset > 0)
        def _():
            back_to(pw_out, pw_in, w_send, w_recv, offset).start()
            back_to(oq_out, oq_in, o_send, o_recv, offset).start()

        return carry

    lax.fori_loop(0, team, attend_unit, 0)
    pw_in[me] = pw_out[me]
    oq_in[me] = oq_out[me]

    def key_grads(at, carry):
        offset = lax.rem(at + 1, team)
        unit = before(offset)
        for half in range(2):
            block = 2 * unit + half
            live = meta_s[unit, half, TMAX]
            total = None
            for slot in range(TMAX):
                other = meta_s[unit, half, slot]
                place = jnp.int32(0)
                for there in range(1, TMAX):
                    same = meta_s[other // 2, other % 2, there] == block
                    place = jnp.where(same, jnp.int32(there), place)
                index = jnp.where(slot < live, other * TMAX + place, blocks * TMAX)
                part = dot(zw_all[index], qg2[other])
                total = part if total is None else total + part
            dkv_out[unit, half] = jnp.where(lane, total * SCALE, total).astype(BF16)

        @pl.when(offset > 0)
        def _():
            back_to(dkv_out, dkv_in, d_send, d_recv, offset).start()

        return carry

    lax.fori_loop(0, team, key_grads, 0)
    dkv_in[me] = dkv_out[me]

    for offset in range(1, team):
        back_to(pw_out, pw_in, w_send, w_recv, offset).wait()
    forwards = []
    for step in range(ROUNDS):
        by = step + 1
        for half in range(2):
            shift = by if half == 0 else clusters - by
            index = step * 2 + half
            copy = remote(
                pw_in.at[:, half],
                pw_far.at[step, 1 - half],
                f_send.at[index],
                f_recv.at[index],
                (lax.rem(row + shift, clusters), me),
            )
            copy.start()
            forwards.append(copy)
    marks = [head_marks(BLOCK, slot, width) for slot in range(2 * ROUNDS)]

    def by_node(flat):
        flat = flat.reshape(8 * HEADS, BLOCK)
        flat = jnp.concatenate([flat, jnp.zeros((BLOCK - 8 * HEADS, BLOCK), F32)], 0)
        return flat.T.astype(BF16)

    def heads_of(buf, half, left):
        parts = [buf[head, half][:, left : left + HEAD_DIM] for head in range(team)]
        return jnp.concatenate(parts, 1).astype(F32)

    for offset in range(1, team):
        back_to(oq_out, oq_in, o_send, o_recv, offset).wait()
    for half in range(2):
        rows = slice(half * BLOCK, (half + 1) * BLOCK)
        turned = by_node(pw_in[:, half])
        attended = heads_of(oq_in, half, HEAD_DIM)
        query_grad = heads_of(oq_in, half, 0)
        for step in range(ROUNDS):
            w = dot(turned, marks[step])
            z = dot(turned, marks[ROUNDS + step]) * SCALE
            attended += w * picked[1, step, rows].astype(F32)
            query_grad += z * picked[0, step, rows].astype(F32)
        out_ref[rows] = attended.astype(BF16)
        dq_ref[rows] = query_grad.astype(BF16)

    for copy in second + forwards:
        copy.wait()
    backs = []
    for half in range(2):
        rows = slice(half * BLOCK, (half + 1) * BLOCK)
        back_key, back_value = None, None
        for step in range(ROUNDS):
            turned = by_node(pw_far[step, half])
            pick = pick_rows(partner_ref[step : step + 1, rows])
            w = dot(turned, marks[step])
            z = dot(turned, marks[ROUNDS + step]) * SCALE
            term_key = (z * far[q_at, step, half].astype(F32)).astype(BF16)
            term_value = (w * far[g_at, step, half].astype(F32)).astype(BF16)
            part_key, part_value = dot(pick, term_key), dot(pick, term_value)
            back_key = part_key if back_key is None else back_key + part_key
            back_value = part_value if back_value is None else back_value + part_value
        backs.append((back_key, back_value))
    for offset in range(1, team):
        back_to(dkv_out, dkv_in, d_send, d_recv, offset).wait()
    for half in range(2):
        rows = slice(half * BLOCK, (half + 1) * BLOCK)
        dk_ref[rows] = (heads_of(dkv_in, half, 0) + backs[half][0]).astype(BF16)
        dv_ref[rows] = (heads_of(dkv_in, half, HEAD_DIM) + backs[half][1]).astype(BF16)


def shards(clusters, team, query, key, value, out_grad, partner, tiles, tile_count):
    nodes, width = query.shape
    meta = jnp.concatenate([tiles, tile_count[:, None]], 1)
    meta = jnp.pad(meta, ((0, 8 - meta.shape[0]), (0, 128 - meta.shape[1])))
    shape = jax.ShapeDtypeStruct
    whole = pl.BlockSpec(memory_space=VMEM)
    dma = pltpu.SemaphoreType.DMA
    blocks = 2 * team
    big = VMEM((team, 2, BLOCK, BLOCK), BF16)
    few = VMEM((team, 2, 8, BLOCK), F32)
    metas = (team, 8, 128)
    return pl.pallas_call(
        functools.partial(fused_kernel, clusters, team),
        out_shape=(shape((nodes, width), BF16),) * 4,
        in_specs=[pl.BlockSpec(memory_space=pl.ANY)] * 4 + [whole] * 2,
        out_specs=(whole,) * 4,
        scratch_shapes=[
            VMEM((4, nodes, width), BF16),
            VMEM((4, ROUNDS, 2, BLOCK, width), BF16),
            big,
            big,
            big,
            big,
            few,
            few,
            VMEM(metas, jnp.int32),
            pltpu.SMEM(metas, jnp.int32),
            VMEM((2, ROUNDS, nodes, width), BF16),
            VMEM((blocks, 2 * BLOCK, BLOCK), BF16),
            VMEM((blocks, BLOCK, BLOCK), BF16),
            VMEM((blocks * TMAX + 1, BLOCK, 2 * BLOCK), BF16),
            big,
            big,
            big,
            big,
            few,
            few,
            VMEM((ROUNDS, 2, team, 8, BLOCK), F32),
            dma((4,)),
            dma,
        ]
        + [dma((team,))] * 14
        + [dma((8 * ROUNDS,))] * 2
        + [dma((2 * ROUNDS,))] * 2,
        compiler_params=pltpu.CompilerParams(
            collective_id=0, has_side_effects=True, vmem_limit_bytes=LIMIT
        ),
    )(query, key, value, out_grad, partner, meta)


def solution(mesh):
    rows = P(("grp", "blk"), None)
    in_specs = (rows, rows, rows, rows, P(None, ("grp", "blk")), rows, P(("grp", "blk")))
    return jax.shard_map(
        functools.partial(shards, mesh.shape["grp"], mesh.shape["blk"]),
        mesh=mesh,
        in_specs=in_specs,
        out_specs=(rows,) * 4,
        check_vma=False,
    )
```

```python
import functools

import jax
import jax.numpy as jnp
from jax import lax
from jax.experimental import pallas as pl
from jax.experimental.pallas import tpu as pltpu
from jax.sharding import PartitionSpec as P

HEADS = 8
HEAD_DIM = 64
BLOCK = 128
TMAX = 6
ROUNDS = 2
NEG_BIG = -1e30
SCALE = HEAD_DIM**-0.5
MESH = pl.DeviceIdType.MESH
VMEM = pltpu.VMEM
F32 = jnp.float32
BF16 = jnp.bfloat16
LIMIT = 56 * 1024 * 1024


def grp_offsets(clusters):
    found = set()
    for step in range(ROUNDS):
        found.add((step + 1) % clusters)
        found.add((-step - 1) % clusters)
    return sorted(found - {0})


def greet(clusters, team, row, me):
    barrier = pltpu.get_barrier_semaphore()
    offsets = grp_offsets(clusters)
    for offset in offsets:
        pl.semaphore_signal(
            barrier,
            inc=1,
            device_id=(lax.rem(row + offset, clusters), me),
            device_id_type=MESH,
        )
    for offset in range(1, team):
        pl.semaphore_signal(
            barrier, inc=1, device_id=(row, lax.rem(me + offset, team)), device_id_type=MESH
        )
    return barrier, len(offsets) + team - 1


def remote(src, dst, send_sem, recv_sem, target):
    return pltpu.make_async_remote_copy(
        src_ref=src,
        dst_ref=dst,
        send_sem=send_sem,
        recv_sem=recv_sem,
        device_id=target,
        device_id_type=MESH,
    )


def head_marks(rows, slot, width):
    at = lax.broadcasted_iota(jnp.int32, (rows, width), 0)
    column = lax.broadcasted_iota(jnp.int32, (rows, width), 1)
    hit = at == (column // HEAD_DIM) * 8 + slot
    return jnp.where(hit, 1.0, 0.0).astype(BF16)


def pick_rows(slots):
    at = lax.broadcasted_iota(jnp.int32, (BLOCK, BLOCK), 0)
    hit = jnp.where(at == jnp.broadcast_to(slots, (BLOCK, BLOCK)), 1.0, 0.0)
    return hit.T.astype(BF16)


def dot_last(left, right):
    return lax.dot_general(left, right, (((1,), (1,)), ((), ())), preferred_element_type=F32)


def dot(left, right):
    return jnp.dot(left, right, preferred_element_type=F32)


def fused_kernel(
    clusters,
    team,
    q_hbm,
    k_hbm,
    v_hbm,
    g_hbm,
    partner_hbm,
    tiles_ref,
    count_ref,
    out_ref,
    dq_ref,
    dk_ref,
    dv_ref,
    near,
    far,
    partner_ref,
    meta_ref,
    qg_out,
    kv_out,
    qg_in,
    kv_in,
    pair_out,
    pair_in,
    meta_in,
    meta_s,
    picked,
    qg2,
    kvt,
    zw_all,
    e_all,
    d_all,
    stats,
    oq_out,
    oq_in,
    dkv_out,
    dkv_in,
    pw_out,
    pw_in,
    pw_far,
    load_sem,
    meta_sem,
    qg_send,
    qg_recv,
    kv_send,
    kv_recv,
    m_send,
    m_recv,
    p_send,
    p_recv,
    o_send,
    o_recv,
    d_send,
    d_recv,
    w_send,
    w_recv,
    g_send,
    g_recv,
    f_send,
    f_recv,
):
    row = lax.axis_index("grp")
    me = lax.axis_index("blk")
    width = q_hbm.shape[1]
    blocks = 2 * team
    barrier, count = greet(clusters, team, row, me)
    q_at, k_at, v_at, g_at = range(4)

    loads = [
        pltpu.make_async_copy(src, near.at[at], load_sem.at[at])
        for at, src in enumerate((q_hbm, k_hbm, v_hbm, g_hbm))
    ]
    loads.append(pltpu.make_async_copy(partner_hbm, partner_ref, load_sem.at[4]))
    for load in loads:
        load.start()
    down = lax.broadcasted_iota(jnp.int32, (8, 128), 0)
    right = lax.broadcasted_iota(jnp.int32, (8, 128), 1)
    meta = jnp.zeros((8, 128), jnp.int32)
    for half in range(2):
        for slot in range(TMAX):
            meta = jnp.where((down == half) & (right == slot), tiles_ref[half, slot], meta)
        meta = jnp.where((down == half) & (right == TMAX), count_ref[half], meta)
    meta_ref[...] = meta
    for load in loads:
        load.wait()

    def after(offset):
        return lax.rem(me + offset, team)

    def before(offset):
        return lax.rem(me + team - offset, team)

    def pack(out, one, two):
        for head in range(team):
            cols = slice(head * HEAD_DIM, (head + 1) * HEAD_DIM)
            for half in range(2):
                rows = slice(half * BLOCK, (half + 1) * BLOCK)
                out[head, half] = jnp.concatenate([near[one, rows, cols], near[two, rows, cols]], 1)

    pack(kv_out, k_at, v_at)
    pl.semaphore_wait(barrier, count)

    def across(out, into, send, recv, offset):
        peer = after(offset)
        return remote(out.at[peer], into.at[me], send.at[offset], recv.at[offset], (row, peer))

    def back_to(out, into, send, recv, offset):
        peer = before(offset)
        return remote(out.at[peer], into.at[me], send.at[offset], recv.at[offset], (row, peer))

    def matched(at, step, half):
        by = step + 1
        shift = by if half == 1 else clusters - by
        index = (at * ROUNDS + step) * 2 + half
        rows = pl.ds((1 - half) * BLOCK, BLOCK)
        return remote(
            near.at[at, rows],
            far.at[at, step, half],
            g_send.at[index],
            g_recv.at[index],
            (lax.rem(row + shift, clusters), me),
        )

    def meta_move(offset):
        peer = after(offset)
        return remote(
            meta_ref, meta_in.at[me], m_send.at[offset], m_recv.at[offset], (row, peer)
        )

    def all_matched(kinds):
        return [matched(at, step, half) for at in kinds for step in range(ROUNDS) for half in range(2)]

    metas = [meta_move(offset) for offset in range(1, team)]
    kv_moves = [across(kv_out, kv_in, kv_send, kv_recv, offset) for offset in range(1, team)]
    qg_moves = [across(qg_out, qg_in, qg_send, qg_recv, offset) for offset in range(1, team)]
    first = all_matched((k_at, v_at))
    second = all_matched((q_at, g_at))
    for copy in metas + first + kv_moves:
        copy.start()
    pack(qg_out, q_at, g_at)
    for copy in qg_moves + second:
        copy.start()
    kv_in[me] = kv_out[me]
    qg_in[me] = qg_out[me]
    meta_in[me] = meta_ref[...]
    zw_all[blocks * TMAX] = jnp.zeros((BLOCK, 2 * BLOCK), BF16)
    for copy in metas:
        copy.wait()
    to_scalar = pltpu.make_async_copy(meta_in, meta_s, meta_sem)
    to_scalar.start()
    to_scalar.wait()
    for copy in kv_moves:
        copy.wait()

    def turn(unit, carry):
        for half in range(2):
            kvt[2 * unit + half] = kv_in[unit, half].astype(F32).T.astype(BF16)
        return carry

    lax.fori_loop(0, team, turn, 0)

    lane = lax.broadcasted_iota(jnp.int32, (BLOCK, BLOCK), 1) < HEAD_DIM

    def attend_local(unit, half):
        block = 2 * unit + half
        qg = qg_in[unit, half].astype(F32)
        split = jnp.concatenate([jnp.where(lane, qg * SCALE, 0.0), jnp.where(lane, 0.0, qg)], 0)
        split = split.astype(BF16)
        qg2[block] = split
        live = meta_s[unit, half, TMAX]
        s_loc = []
        top = None
        for slot in range(TMAX):
            source = meta_s[unit, half, slot]
            both = dot_last(kv_in[source // 2, source % 2], split)
            scores = both[:, :BLOCK] + jnp.where(slot < live, 0.0, NEG_BIG)
            s_loc.append(scores)
            d_all[block * TMAX + slot] = both[:, BLOCK:]
            most = jnp.max(scores, 0, keepdims=True)
            top = most if top is None else jnp.maximum(top, most)
        total, weighted = None, None
        for slot in range(TMAX):
            e = jnp.exp(s_loc[slot] - top)
            e_all[block * TMAX + slot] = e
            part = jnp.sum(e, 0, keepdims=True)
            other = jnp.sum(e * d_all[block * TMAX + slot], 0, keepdims=True)
            total = part if total is None else total + part
            weighted = other if weighted is None else weighted + other
        stats[block] = jnp.concatenate(
            [top, total, weighted, jnp.zeros((5, BLOCK), F32)], 0
        )

    def local_unit(offset, carry):
        unit = before(offset)

        @pl.when(offset > 0)
        def _():
            across(qg_out, qg_in, qg_send, qg_recv, offset).wait()

        for half in range(2):
            attend_local(unit, half)
        return carry

    lax.fori_loop(0, team // 2, local_unit, 0)

    for copy in first:
        copy.wait()
    marks = [head_marks(8 * HEADS, slot, width) for slot in range(2 * ROUNDS)]
    for half in range(2):
        rows = slice(half * BLOCK, (half + 1) * BLOCK)
        total = None
        for step in range(ROUNDS):
            pick = pick_rows(partner_ref[step : step + 1, rows])
            for at, (kind, own) in enumerate(((k_at, q_at), (v_at, g_at))):
                taken = dot(pick, far[kind, step, half])
                picked[at, step, rows] = taken.astype(BF16)
                product = near[own, rows].astype(F32) * taken
                high = product.astype(BF16)
                low = (product - high.astype(F32)).astype(BF16)
                mark = marks[at * ROUNDS + step]
                part = dot_last(mark, high) + dot_last(mark, low)
                total = part if total is None else total + part
        pair_out[:, half] = total.reshape(HEADS, 8, BLOCK)
    pairs = [across(pair_out, pair_in, p_send, p_recv, offset) for offset in range(1, team)]
    for copy in pairs:
        copy.start()
    pair_in[me] = pair_out[me]

    lax.fori_loop(team // 2, team, local_unit, 0)

    def attend_pair(unit, half):
        block = 2 * unit + half
        ids = [meta_s[unit, half, slot] for slot in range(TMAX)]
        held = stats[block]
        top_loc, total_loc, dot_loc = held[0:1], held[1:2], held[2:3]
        pair = pair_in[unit, half]
        s_pair = [pair[r : r + 1] * SCALE for r in range(ROUNDS)]
        d_pair = [pair[ROUNDS + r : ROUNDS + r + 1] for r in range(ROUNDS)]
        top = functools.reduce(jnp.maximum, s_pair, top_loc)
        shrink = jnp.exp(top_loc - top)
        e_pair = [jnp.exp(s - top) for s in s_pair]
        inverse = 1.0 / functools.reduce(jnp.add, e_pair, total_loc * shrink)
        factor = shrink * inverse
        p_pair = [e * inverse for e in e_pair]
        delta = functools.reduce(
            jnp.add, [p * d for p, d in zip(p_pair, d_pair)], dot_loc * factor
        )
        w_pair = [p.astype(BF16).astype(F32) for p in p_pair]
        z_pair = [(p * (d - delta)).astype(BF16).astype(F32) for p, d in zip(p_pair, d_pair)]
        pw_out[unit, half] = jnp.concatenate(
            w_pair + z_pair + [jnp.zeros((8 - 2 * ROUNDS, BLOCK), F32)], 0
        )
        back = None
        for slot in range(TMAX):
            p = e_all[block * TMAX + slot] * factor
            z = (p * (d_all[block * TMAX + slot] - delta)).astype(BF16)
            zw = jnp.concatenate([z, p.astype(BF16)], 1)
            zw_all[block * TMAX + slot] = zw
            part = dot(kvt[ids[slot]], zw)
            back = part if back is None else back + part
        turned = jnp.concatenate([back[:HEAD_DIM, :BLOCK] * SCALE, back[HEAD_DIM:, BLOCK:]], 0)
        oq_out[unit, half] = turned.T.astype(BF16)

    def attend_unit(offset, carry):
        unit = before(offset)

        @pl.when(offset > 0)
        def _():
            across(pair_out, pair_in, p_send, p_recv, offset).wait()

        for half in range(2):
            attend_pair(unit, half)

        @pl.when(offset > 0)
        def _():
            back_to(pw_out, pw_in, w_send, w_recv, offset).start()
            back_to(oq_out, oq_in, o_send, o_recv, offset).start()

        return carry

    lax.fori_loop(0, team, attend_unit, 0)
    pw_in[me] = pw_out[me]
    oq_in[me] = oq_out[me]

    def key_grads(at, carry):
        offset = lax.rem(at + 1, team)
        unit = before(offset)
        for half in range(2):
            block = 2 * unit + half
            live = meta_s[unit, half, TMAX]
            total = None
            for slot in range(TMAX):
                other = meta_s[unit, half, slot]
                place = jnp.int32(0)
                for there in range(1, TMAX):
                    same = meta_s[other // 2, other % 2, there] == block
                    place = jnp.where(same, jnp.int32(there), place)
                index = jnp.where(slot < live, other * TMAX + place, blocks * TMAX)
                part = dot(zw_all[index], qg2[other])
                total = part if total is None else total + part
            dkv_out[unit, half] = total.astype(BF16)

        @pl.when(offset > 0)
        def _():
            back_to(dkv_out, dkv_in, d_send, d_recv, offset).start()

        return carry

    lax.fori_loop(0, team, key_grads, 0)
    dkv_in[me] = dkv_out[me]

    for offset in range(1, team):
        back_to(pw_out, pw_in, w_send, w_recv, offset).wait()
    forwards = []
    for step in range(ROUNDS):
        by = step + 1
        for half in range(2):
            shift = by if half == 0 else clusters - by
            index = step * 2 + half
            copy = remote(
                pw_in.at[:, half],
                pw_far.at[step, 1 - half],
                f_send.at[index],
                f_recv.at[index],
                (lax.rem(row + shift, clusters), me),
            )
            copy.start()
            forwards.append(copy)
    marks = [head_marks(BLOCK, slot, width) for slot in range(2 * ROUNDS)]

    def by_node(flat):
        flat = flat.reshape(8 * HEADS, BLOCK)
        flat = jnp.concatenate([flat, jnp.zeros((BLOCK - 8 * HEADS, BLOCK), F32)], 0)
        return flat.T.astype(BF16)

    def heads_of(buf, half, left):
        parts = [buf[head, half][:, left : left + HEAD_DIM] for head in range(team)]
        return jnp.concatenate(parts, 1).astype(F32)

    for offset in range(1, team):
        back_to(oq_out, oq_in, o_send, o_recv, offset).wait()
    for half in range(2):
        rows = slice(half * BLOCK, (half + 1) * BLOCK)
        turned = by_node(pw_in[:, half])
        attended = heads_of(oq_in, half, HEAD_DIM)
        query_grad = heads_of(oq_in, half, 0)
        for step in range(ROUNDS):
            w = dot(turned, marks[step])
            z = dot(turned, marks[ROUNDS + step]) * SCALE
            attended += w * picked[1, step, rows].astype(F32)
            query_grad += z * picked[0, step, rows].astype(F32)
        out_ref[rows] = attended.astype(BF16)
        dq_ref[rows] = query_grad.astype(BF16)

    for copy in second + forwards:
        copy.wait()
    backs = []
    for half in range(2):
        rows = slice(half * BLOCK, (half + 1) * BLOCK)
        back_key, back_value = None, None
        for step in range(ROUNDS):
            turned = by_node(pw_far[step, half])
            pick = pick_rows(partner_ref[step : step + 1, rows])
            w = dot(turned, marks[step])
            z = dot(turned, marks[ROUNDS + step]) * SCALE
            term_key = (z * far[q_at, step, half].astype(F32)).astype(BF16)
            term_value = (w * far[g_at, step, half].astype(F32)).astype(BF16)
            part_key, part_value = dot(pick, term_key), dot(pick, term_value)
            back_key = part_key if back_key is None else back_key + part_key
            back_value = part_value if back_value is None else back_value + part_value
        backs.append((back_key, back_value))
    for offset in range(1, team):
        back_to(dkv_out, dkv_in, d_send, d_recv, offset).wait()
    for half in range(2):
        rows = slice(half * BLOCK, (half + 1) * BLOCK)
        dk_ref[rows] = (heads_of(dkv_in, half, 0) + backs[half][0]).astype(BF16)
        dv_ref[rows] = (heads_of(dkv_in, half, HEAD_DIM) + backs[half][1]).astype(BF16)


def write_kernel(*refs):
    sems = refs[8]
    copies = [pltpu.make_async_copy(refs[at], refs[4 + at], sems.at[at]) for at in range(4)]
    for copy in copies:
        copy.start()
    for copy in copies:
        copy.wait()


def shards(clusters, team, query, key, value, out_grad, partner, tiles, tile_count):
    nodes, width = query.shape
    shape = jax.ShapeDtypeStruct
    whole = pl.BlockSpec(memory_space=VMEM)
    scalar = pl.BlockSpec(memory_space=pltpu.SMEM)
    anywhere = pl.BlockSpec(memory_space=pl.ANY)
    dma = pltpu.SemaphoreType.DMA
    blocks = 2 * team
    big = VMEM((team, 2, BLOCK, BLOCK), BF16)
    few = VMEM((team, 2, 8, BLOCK), F32)
    metas = (team, 8, 128)
    results = pl.pallas_call(
        functools.partial(fused_kernel, clusters, team),
        out_shape=(shape((nodes, width), BF16),) * 4,
        in_specs=[anywhere] * 5 + [scalar] * 2,
        out_specs=(whole,) * 4,
        scratch_shapes=[
            VMEM((4, nodes, width), BF16),
            VMEM((4, ROUNDS, 2, BLOCK, width), BF16),
            VMEM((ROUNDS, nodes), jnp.int32),
            VMEM((8, 128), jnp.int32),
            big,
            big,
            big,
            big,
            few,
            few,
            VMEM(metas, jnp.int32),
            pltpu.SMEM(metas, jnp.int32),
            VMEM((2, ROUNDS, nodes, width), BF16),
            VMEM((blocks, 2 * BLOCK, BLOCK), BF16),
            VMEM((blocks, BLOCK, BLOCK), BF16),
            VMEM((blocks * TMAX + 1, BLOCK, 2 * BLOCK), BF16),
            VMEM((blocks * TMAX, BLOCK, BLOCK), F32),
            VMEM((blocks * TMAX, BLOCK, BLOCK), F32),
            VMEM((blocks, 8, BLOCK), F32),
            big,
            big,
            big,
            big,
            few,
            few,
            VMEM((ROUNDS, 2, team, 8, BLOCK), F32),
            dma((5,)),
            dma,
        ]
        + [dma((team,))] * 14
        + [dma((8 * ROUNDS,))] * 2
        + [dma((2 * ROUNDS,))] * 2,
        compiler_params=pltpu.CompilerParams(
            collective_id=0, has_side_effects=True, vmem_limit_bytes=LIMIT
        ),
    )(query, key, value, out_grad, partner, tiles, tile_count)
    return pl.pallas_call(
        write_kernel,
        out_shape=(shape((nodes, width), BF16),) * 4,
        in_specs=[anywhere] * 4,
        out_specs=(anywhere,) * 4,
        scratch_shapes=[dma((4,))],
    )(*results)


def solution(mesh):
    rows = P(("grp", "blk"), None)
    in_specs = (rows, rows, rows, rows, P(None, ("grp", "blk")), rows, P(("grp", "blk")))
    return jax.shard_map(
        functools.partial(shards, mesh.shape["grp"], mesh.shape["blk"]),
        mesh=mesh,
        in_specs=in_specs,
        out_specs=(rows,) * 4,
        check_vma=False,
    )
```

```python
import functools

import jax
import jax.numpy as jnp
from jax import lax
from jax.experimental import pallas as pl
from jax.experimental.pallas import tpu as pltpu
from jax.sharding import PartitionSpec as P

HEADS = 8
HEAD_DIM = 64
BLOCK = 128
TMAX = 6
ROUNDS = 2
NEG_BIG = -1e30
SCALE = HEAD_DIM**-0.5
MESH = pl.DeviceIdType.MESH
VMEM = pltpu.VMEM
F32 = jnp.float32
BF16 = jnp.bfloat16
LIMIT = 56 * 1024 * 1024


def grp_offsets(clusters):
    found = set()
    for step in range(ROUNDS):
        found.add((step + 1) % clusters)
        found.add((-step - 1) % clusters)
    return sorted(found - {0})


def greet(clusters, team, row, me):
    barrier = pltpu.get_barrier_semaphore()
    offsets = grp_offsets(clusters)
    for offset in offsets:
        pl.semaphore_signal(
            barrier,
            inc=1,
            device_id=(lax.rem(row + offset, clusters), me),
            device_id_type=MESH,
        )
    for offset in range(1, team):
        pl.semaphore_signal(
            barrier, inc=1, device_id=(row, lax.rem(me + offset, team)), device_id_type=MESH
        )
    return barrier, len(offsets) + team - 1


def remote(src, dst, send_sem, recv_sem, target):
    return pltpu.make_async_remote_copy(
        src_ref=src,
        dst_ref=dst,
        send_sem=send_sem,
        recv_sem=recv_sem,
        device_id=target,
        device_id_type=MESH,
    )


def head_marks(rows, slot, width):
    at = lax.broadcasted_iota(jnp.int32, (rows, width), 0)
    column = lax.broadcasted_iota(jnp.int32, (rows, width), 1)
    hit = at == (column // HEAD_DIM) * 8 + slot
    return jnp.where(hit, 1.0, 0.0).astype(BF16)


def pick_rows(slots):
    at = lax.broadcasted_iota(jnp.int32, (BLOCK, BLOCK), 0)
    hit = jnp.where(at == jnp.broadcast_to(slots, (BLOCK, BLOCK)), 1.0, 0.0)
    return hit.T.astype(BF16)


def dot_last(left, right):
    return lax.dot_general(left, right, (((1,), (1,)), ((), ())), preferred_element_type=F32)


def dot(left, right):
    return jnp.dot(left, right, preferred_element_type=F32)


def fused_kernel(
    clusters,
    team,
    q_hbm,
    k_hbm,
    v_hbm,
    g_hbm,
    partner_hbm,
    tiles_ref,
    count_ref,
    out_ref,
    dq_ref,
    dk_ref,
    dv_ref,
    near,
    far,
    partner_ref,
    meta_ref,
    qg_out,
    kv_out,
    qg_in,
    kv_in,
    pair_out,
    pair_in,
    meta_in,
    meta_s,
    picked,
    qg2,
    kvt,
    zw_all,
    e_all,
    d_all,
    stats,
    oq_out,
    oq_in,
    dkv_out,
    dkv_in,
    pw_out,
    pw_in,
    pw_far,
    load_sem,
    meta_sem,
    qg_send,
    qg_recv,
    kv_send,
    kv_recv,
    m_send,
    m_recv,
    p_send,
    p_recv,
    o_send,
    o_recv,
    d_send,
    d_recv,
    w_send,
    w_recv,
    g_send,
    g_recv,
    f_send,
    f_recv,
):
    row = lax.axis_index("grp")
    me = lax.axis_index("blk")
    width = q_hbm.shape[1]
    blocks = 2 * team
    barrier, count = greet(clusters, team, row, me)
    q_at, k_at, v_at, g_at = range(4)

    loads = [
        pltpu.make_async_copy(src, near.at[at], load_sem.at[at])
        for at, src in enumerate((q_hbm, k_hbm, v_hbm, g_hbm))
    ]
    loads.append(pltpu.make_async_copy(partner_hbm, partner_ref, load_sem.at[4]))
    for load in loads:
        load.start()
    down = lax.broadcasted_iota(jnp.int32, (8, 128), 0)
    right = lax.broadcasted_iota(jnp.int32, (8, 128), 1)
    meta = jnp.zeros((8, 128), jnp.int32)
    for half in range(2):
        for slot in range(TMAX):
            meta = jnp.where((down == half) & (right == slot), tiles_ref[half, slot], meta)
        meta = jnp.where((down == half) & (right == TMAX), count_ref[half], meta)
    meta_ref[...] = meta
    for load in loads:
        load.wait()

    def after(offset):
        return lax.rem(me + offset, team)

    def before(offset):
        return lax.rem(me + team - offset, team)

    def pack(out, one, two):
        for head in range(team):
            cols = slice(head * HEAD_DIM, (head + 1) * HEAD_DIM)
            for half in range(2):
                rows = slice(half * BLOCK, (half + 1) * BLOCK)
                out[head, half] = jnp.concatenate([near[one, rows, cols], near[two, rows, cols]], 1)

    pack(kv_out, k_at, v_at)
    pl.semaphore_wait(barrier, count)

    def across(out, into, send, recv, offset):
        peer = after(offset)
        return remote(out.at[peer], into.at[me], send.at[offset], recv.at[offset], (row, peer))

    def back_to(out, into, send, recv, offset):
        peer = before(offset)
        return remote(out.at[peer], into.at[me], send.at[offset], recv.at[offset], (row, peer))

    def matched(at, step, half):
        by = step + 1
        shift = by if half == 1 else clusters - by
        index = (at * ROUNDS + step) * 2 + half
        rows = pl.ds((1 - half) * BLOCK, BLOCK)
        return remote(
            near.at[at, rows],
            far.at[at, step, half],
            g_send.at[index],
            g_recv.at[index],
            (lax.rem(row + shift, clusters), me),
        )

    def meta_move(offset):
        peer = after(offset)
        return remote(
            meta_ref, meta_in.at[me], m_send.at[offset], m_recv.at[offset], (row, peer)
        )

    def all_matched(kinds):
        return [matched(at, step, half) for at in kinds for step in range(ROUNDS) for half in range(2)]

    metas = [meta_move(offset) for offset in range(1, team)]
    kv_moves = [across(kv_out, kv_in, kv_send, kv_recv, offset) for offset in range(1, team)]
    qg_moves = [across(qg_out, qg_in, qg_send, qg_recv, offset) for offset in range(1, team)]
    first = all_matched((k_at, v_at))
    second = all_matched((q_at, g_at))
    for copy in metas + first + kv_moves:
        copy.start()
    pack(qg_out, q_at, g_at)
    for copy in qg_moves:
        copy.start()
    kv_in[me] = kv_out[me]
    qg_in[me] = qg_out[me]
    meta_in[me] = meta_ref[...]
    zw_all[blocks * TMAX] = jnp.zeros((BLOCK, 2 * BLOCK), BF16)
    for copy in metas:
        copy.wait()
    to_scalar = pltpu.make_async_copy(meta_in, meta_s, meta_sem)
    to_scalar.start()
    to_scalar.wait()
    for copy in kv_moves:
        copy.wait()

    def turn(unit, carry):
        for half in range(2):
            kvt[2 * unit + half] = kv_in[unit, half].astype(F32).T.astype(BF16)
        return carry

    lax.fori_loop(0, team, turn, 0)

    lane = lax.broadcasted_iota(jnp.int32, (BLOCK, BLOCK), 1) < HEAD_DIM

    def attend_local(unit, half):
        block = 2 * unit + half
        qg = qg_in[unit, half].astype(F32)
        split = jnp.concatenate([jnp.where(lane, qg * SCALE, 0.0), jnp.where(lane, 0.0, qg)], 0)
        split = split.astype(BF16)
        qg2[block] = split
        live = meta_s[unit, half, TMAX]
        s_loc = []
        top = None
        for slot in range(TMAX):
            source = meta_s[unit, half, slot]
            both = dot_last(kv_in[source // 2, source % 2], split)
            scores = both[:, :BLOCK] + jnp.where(slot < live, 0.0, NEG_BIG)
            s_loc.append(scores)
            d_all[block * TMAX + slot] = both[:, BLOCK:]
            most = jnp.max(scores, 0, keepdims=True)
            top = most if top is None else jnp.maximum(top, most)
        total, weighted = None, None
        for slot in range(TMAX):
            e = jnp.exp(s_loc[slot] - top)
            e_all[block * TMAX + slot] = e
            part = jnp.sum(e, 0, keepdims=True)
            other = jnp.sum(e * d_all[block * TMAX + slot], 0, keepdims=True)
            total = part if total is None else total + part
            weighted = other if weighted is None else weighted + other
        stats[block] = jnp.concatenate(
            [top, total, weighted, jnp.zeros((5, BLOCK), F32)], 0
        )

    for half in range(2):
        attend_local(me, half)

    for copy in first:
        copy.wait()
    for copy in second:
        copy.start()
    marks = [head_marks(8 * HEADS, slot, width) for slot in range(2 * ROUNDS)]
    for half in range(2):
        rows = slice(half * BLOCK, (half + 1) * BLOCK)
        total = None
        for step in range(ROUNDS):
            pick = pick_rows(partner_ref[step : step + 1, rows])
            for at, (kind, own) in enumerate(((k_at, q_at), (v_at, g_at))):
                taken = dot(pick, far[kind, step, half])
                picked[at, step, rows] = taken.astype(BF16)
                product = near[own, rows].astype(F32) * taken
                high = product.astype(BF16)
                low = (product - high.astype(F32)).astype(BF16)
                mark = marks[at * ROUNDS + step]
                part = dot_last(mark, high) + dot_last(mark, low)
                total = part if total is None else total + part
        pair_out[:, half] = total.reshape(HEADS, 8, BLOCK)
    pairs = [across(pair_out, pair_in, p_send, p_recv, offset) for offset in range(1, team)]
    for copy in pairs:
        copy.start()
    pair_in[me] = pair_out[me]

    def attend_pair(unit, half):
        block = 2 * unit + half
        ids = [meta_s[unit, half, slot] for slot in range(TMAX)]
        held = stats[block]
        top_loc, total_loc, dot_loc = held[0:1], held[1:2], held[2:3]
        pair = pair_in[unit, half]
        s_pair = [pair[r : r + 1] * SCALE for r in range(ROUNDS)]
        d_pair = [pair[ROUNDS + r : ROUNDS + r + 1] for r in range(ROUNDS)]
        top = functools.reduce(jnp.maximum, s_pair, top_loc)
        shrink = jnp.exp(top_loc - top)
        e_pair = [jnp.exp(s - top) for s in s_pair]
        inverse = 1.0 / functools.reduce(jnp.add, e_pair, total_loc * shrink)
        factor = shrink * inverse
        p_pair = [e * inverse for e in e_pair]
        delta = functools.reduce(
            jnp.add, [p * d for p, d in zip(p_pair, d_pair)], dot_loc * factor
        )
        w_pair = [p.astype(BF16).astype(F32) for p in p_pair]
        z_pair = [(p * (d - delta)).astype(BF16).astype(F32) for p, d in zip(p_pair, d_pair)]
        pw_out[unit, half] = jnp.concatenate(
            w_pair + z_pair + [jnp.zeros((8 - 2 * ROUNDS, BLOCK), F32)], 0
        )
        back = None
        for slot in range(TMAX):
            p = e_all[block * TMAX + slot] * factor
            z = (p * (d_all[block * TMAX + slot] - delta)).astype(BF16)
            zw = jnp.concatenate([z, p.astype(BF16)], 1)
            zw_all[block * TMAX + slot] = zw
            part = dot(kvt[ids[slot]], zw)
            back = part if back is None else back + part
        turned = jnp.concatenate([back[:HEAD_DIM, :BLOCK] * SCALE, back[HEAD_DIM:, BLOCK:]], 0)
        oq_out[unit, half] = turned.T.astype(BF16)

    def attend_unit(offset, carry):
        unit = before(offset)

        @pl.when(offset > 0)
        def _():
            across(qg_out, qg_in, qg_send, qg_recv, offset).wait()
            for half in range(2):
                attend_local(unit, half)
            across(pair_out, pair_in, p_send, p_recv, offset).wait()

        for half in range(2):
            attend_pair(unit, half)

        @pl.when(offset > 0)
        def _():
            back_to(pw_out, pw_in, w_send, w_recv, offset).start()
            back_to(oq_out, oq_in, o_send, o_recv, offset).start()

        return carry

    lax.fori_loop(0, team, attend_unit, 0)
    pw_in[me] = pw_out[me]
    oq_in[me] = oq_out[me]

    def key_grads(at, carry):
        offset = lax.rem(at + 1, team)
        unit = before(offset)
        for half in range(2):
            block = 2 * unit + half
            live = meta_s[unit, half, TMAX]
            total = None
            for slot in range(TMAX):
                other = meta_s[unit, half, slot]
                place = jnp.int32(0)
                for there in range(1, TMAX):
                    same = meta_s[other // 2, other % 2, there] == block
                    place = jnp.where(same, jnp.int32(there), place)
                index = jnp.where(slot < live, other * TMAX + place, blocks * TMAX)
                part = dot(zw_all[index], qg2[other])
                total = part if total is None else total + part
            dkv_out[unit, half] = total.astype(BF16)

        @pl.when(offset > 0)
        def _():
            back_to(dkv_out, dkv_in, d_send, d_recv, offset).start()

        return carry

    lax.fori_loop(0, team, key_grads, 0)
    dkv_in[me] = dkv_out[me]

    for offset in range(1, team):
        back_to(pw_out, pw_in, w_send, w_recv, offset).wait()
    forwards = []
    for step in range(ROUNDS):
        by = step + 1
        for half in range(2):
            shift = by if half == 0 else clusters - by
            index = step * 2 + half
            copy = remote(
                pw_in.at[:, half],
                pw_far.at[step, 1 - half],
                f_send.at[index],
                f_recv.at[index],
                (lax.rem(row + shift, clusters), me),
            )
            copy.start()
            forwards.append(copy)
    marks = [head_marks(BLOCK, slot, width) for slot in range(2 * ROUNDS)]

    def by_node(flat):
        flat = flat.reshape(8 * HEADS, BLOCK)
        flat = jnp.concatenate([flat, jnp.zeros((BLOCK - 8 * HEADS, BLOCK), F32)], 0)
        return flat.T.astype(BF16)

    def heads_of(buf, half, left):
        parts = [buf[head, half][:, left : left + HEAD_DIM] for head in range(team)]
        return jnp.concatenate(parts, 1).astype(F32)

    for offset in range(1, team):
        back_to(oq_out, oq_in, o_send, o_recv, offset).wait()
    for half in range(2):
        rows = slice(half * BLOCK, (half + 1) * BLOCK)
        turned = by_node(pw_in[:, half])
        attended = heads_of(oq_in, half, HEAD_DIM)
        query_grad = heads_of(oq_in, half, 0)
        for step in range(ROUNDS):
            w = dot(turned, marks[step])
            z = dot(turned, marks[ROUNDS + step]) * SCALE
            attended += w * picked[1, step, rows].astype(F32)
            query_grad += z * picked[0, step, rows].astype(F32)
        out_ref[rows] = attended.astype(BF16)
        dq_ref[rows] = query_grad.astype(BF16)

    for copy in second + forwards:
        copy.wait()
    backs = []
    for half in range(2):
        rows = slice(half * BLOCK, (half + 1) * BLOCK)
        back_key, back_value = None, None
        for step in range(ROUNDS):
            turned = by_node(pw_far[step, half])
            pick = pick_rows(partner_ref[step : step + 1, rows])
            w = dot(turned, marks[step])
            z = dot(turned, marks[ROUNDS + step]) * SCALE
            term_key = (z * far[q_at, step, half].astype(F32)).astype(BF16)
            term_value = (w * far[g_at, step, half].astype(F32)).astype(BF16)
            part_key, part_value = dot(pick, term_key), dot(pick, term_value)
            back_key = part_key if back_key is None else back_key + part_key
            back_value = part_value if back_value is None else back_value + part_value
        backs.append((back_key, back_value))
    for offset in range(1, team):
        back_to(dkv_out, dkv_in, d_send, d_recv, offset).wait()
    for half in range(2):
        rows = slice(half * BLOCK, (half + 1) * BLOCK)
        dk_ref[rows] = (heads_of(dkv_in, half, 0) + backs[half][0]).astype(BF16)
        dv_ref[rows] = (heads_of(dkv_in, half, HEAD_DIM) + backs[half][1]).astype(BF16)


def write_kernel(*refs):
    held, in_sems, out_sems = refs[8:]
    copies = [pltpu.make_async_copy(refs[at], held.at[at], in_sems.at[at]) for at in range(4)]
    writes = [pltpu.make_async_copy(held.at[at], refs[4 + at], out_sems.at[at]) for at in range(4)]
    for copy in copies:
        copy.start()
    for copy, write in zip(copies, writes):
        copy.wait()
        write.start()
    for write in writes:
        write.wait()


def shards(clusters, team, query, key, value, out_grad, partner, tiles, tile_count):
    nodes, width = query.shape
    shape = jax.ShapeDtypeStruct
    whole = pl.BlockSpec(memory_space=VMEM)
    scalar = pl.BlockSpec(memory_space=pltpu.SMEM)
    anywhere = pl.BlockSpec(memory_space=pl.ANY)
    dma = pltpu.SemaphoreType.DMA
    blocks = 2 * team
    big = VMEM((team, 2, BLOCK, BLOCK), BF16)
    few = VMEM((team, 2, 8, BLOCK), F32)
    metas = (team, 8, 128)
    results = pl.pallas_call(
        functools.partial(fused_kernel, clusters, team),
        out_shape=(shape((nodes, width), BF16),) * 4,
        in_specs=[anywhere] * 5 + [scalar] * 2,
        out_specs=(whole,) * 4,
        scratch_shapes=[
            VMEM((4, nodes, width), BF16),
            VMEM((4, ROUNDS, 2, BLOCK, width), BF16),
            VMEM((ROUNDS, nodes), jnp.int32),
            VMEM((8, 128), jnp.int32),
            big,
            big,
            big,
            big,
            few,
            few,
            VMEM(metas, jnp.int32),
            pltpu.SMEM(metas, jnp.int32),
            VMEM((2, ROUNDS, nodes, width), BF16),
            VMEM((blocks, 2 * BLOCK, BLOCK), BF16),
            VMEM((blocks, BLOCK, BLOCK), BF16),
            VMEM((blocks * TMAX + 1, BLOCK, 2 * BLOCK), BF16),
            VMEM((blocks * TMAX, BLOCK, BLOCK), F32),
            VMEM((blocks * TMAX, BLOCK, BLOCK), F32),
            VMEM((blocks, 8, BLOCK), F32),
            big,
            big,
            big,
            big,
            few,
            few,
            VMEM((ROUNDS, 2, team, 8, BLOCK), F32),
            dma((5,)),
            dma,
        ]
        + [dma((team,))] * 14
        + [dma((8 * ROUNDS,))] * 2
        + [dma((2 * ROUNDS,))] * 2,
        compiler_params=pltpu.CompilerParams(
            collective_id=0, has_side_effects=True, vmem_limit_bytes=LIMIT
        ),
    )(query, key, value, out_grad, partner, tiles, tile_count)
    return pl.pallas_call(
        write_kernel,
        out_shape=(shape((nodes, width), BF16),) * 4,
        in_specs=[anywhere] * 4,
        out_specs=(anywhere,) * 4,
        scratch_shapes=[VMEM((4, nodes, width), BF16), dma((4,)), dma((4,))],
    )(*results)


def solution(mesh):
    rows = P(("grp", "blk"), None)
    in_specs = (rows, rows, rows, rows, P(None, ("grp", "blk")), rows, P(("grp", "blk")))
    return jax.shard_map(
        functools.partial(shards, mesh.shape["grp"], mesh.shape["blk"]),
        mesh=mesh,
        in_specs=in_specs,
        out_specs=(rows,) * 4,
        check_vma=False,
    )
```

```python
import functools

import jax
import jax.numpy as jnp
from jax import lax
from jax.experimental import pallas as pl
from jax.experimental.pallas import tpu as pltpu
from jax.sharding import PartitionSpec as P

HEADS = 8
HEAD_DIM = 64
BLOCK = 128
TMAX = 6
ROUNDS = 2
NEG_BIG = -1e30
SCALE = HEAD_DIM**-0.5
MESH = pl.DeviceIdType.MESH
VMEM = pltpu.VMEM
F32 = jnp.float32
BF16 = jnp.bfloat16
LIMIT = 56 * 1024 * 1024


def grp_offsets(clusters):
    found = set()
    for step in range(ROUNDS):
        found.add((step + 1) % clusters)
        found.add((-step - 1) % clusters)
    return sorted(found - {0})


def greet(clusters, team, row, me):
    barrier = pltpu.get_barrier_semaphore()
    offsets = grp_offsets(clusters)
    for offset in offsets:
        pl.semaphore_signal(
            barrier,
            inc=1,
            device_id=(lax.rem(row + offset, clusters), me),
            device_id_type=MESH,
        )
    for offset in range(1, team):
        pl.semaphore_signal(
            barrier, inc=1, device_id=(row, lax.rem(me + offset, team)), device_id_type=MESH
        )
    return barrier, len(offsets) + team - 1


def remote(src, dst, send_sem, recv_sem, target):
    return pltpu.make_async_remote_copy(
        src_ref=src,
        dst_ref=dst,
        send_sem=send_sem,
        recv_sem=recv_sem,
        device_id=target,
        device_id_type=MESH,
    )


def head_marks(rows, slot, width):
    at = lax.broadcasted_iota(jnp.int32, (rows, width), 0)
    column = lax.broadcasted_iota(jnp.int32, (rows, width), 1)
    hit = at == (column // HEAD_DIM) * 8 + slot
    return jnp.where(hit, 1.0, 0.0).astype(BF16)


def pick_rows(slots):
    at = lax.broadcasted_iota(jnp.int32, (BLOCK, BLOCK), 0)
    hit = jnp.where(at == jnp.broadcast_to(slots, (BLOCK, BLOCK)), 1.0, 0.0)
    return hit.T.astype(BF16)


def dot_last(left, right):
    return lax.dot_general(left, right, (((1,), (1,)), ((), ())), preferred_element_type=F32)


def dot(left, right):
    return jnp.dot(left, right, preferred_element_type=F32)


def fused_kernel(
    clusters,
    team,
    q_hbm,
    k_hbm,
    v_hbm,
    g_hbm,
    partner_hbm,
    tiles_ref,
    count_ref,
    out_ref,
    dq_ref,
    dk_ref,
    dv_ref,
    near,
    far,
    partner_ref,
    meta_ref,
    qg_out,
    kv_out,
    qg_in,
    kv_in,
    pair_out,
    pair_in,
    meta_in,
    meta_s,
    picked,
    qg2,
    kvt,
    zw_all,
    e_all,
    d_all,
    stats,
    oq_out,
    oq_in,
    dkv_out,
    dkv_in,
    pw_out,
    pw_in,
    pw_far,
    load_sem,
    meta_sem,
    qg_send,
    qg_recv,
    kv_send,
    kv_recv,
    m_send,
    m_recv,
    p_send,
    p_recv,
    o_send,
    o_recv,
    d_send,
    d_recv,
    w_send,
    w_recv,
    g_send,
    g_recv,
    f_send,
    f_recv,
):
    row = lax.axis_index("grp")
    me = lax.axis_index("blk")
    width = q_hbm.shape[1]
    blocks = 2 * team
    barrier, count = greet(clusters, team, row, me)
    q_at, k_at, v_at, g_at = range(4)

    loads = [
        pltpu.make_async_copy(src, near.at[at], load_sem.at[at])
        for at, src in enumerate((q_hbm, k_hbm, v_hbm, g_hbm))
    ]
    loads.append(pltpu.make_async_copy(partner_hbm, partner_ref, load_sem.at[4]))
    for load in loads:
        load.start()
    down = lax.broadcasted_iota(jnp.int32, (8, 128), 0)
    right = lax.broadcasted_iota(jnp.int32, (8, 128), 1)
    meta = jnp.zeros((8, 128), jnp.int32)
    for half in range(2):
        for slot in range(TMAX):
            meta = jnp.where((down == half) & (right == slot), tiles_ref[half, slot], meta)
        meta = jnp.where((down == half) & (right == TMAX), count_ref[half], meta)
    meta_ref[...] = meta
    for load in loads:
        load.wait()

    def after(offset):
        peer, bit = 0, 1
        while bit < team:
            peer = peer + bit * ((me // bit + offset // bit) % 2)
            bit *= 2
        return peer

    before = after

    def pack(out, one, two):
        for head in range(team):
            cols = slice(head * HEAD_DIM, (head + 1) * HEAD_DIM)
            for half in range(2):
                rows = slice(half * BLOCK, (half + 1) * BLOCK)
                out[head, half] = jnp.concatenate([near[one, rows, cols], near[two, rows, cols]], 1)

    pack(kv_out, k_at, v_at)
    pl.semaphore_wait(barrier, count)

    def across(out, into, send, recv, offset):
        peer = after(offset)
        return remote(out.at[peer], into.at[me], send.at[offset], recv.at[offset], (row, peer))

    def back_to(out, into, send, recv, offset):
        peer = before(offset)
        return remote(out.at[peer], into.at[me], send.at[offset], recv.at[offset], (row, peer))

    def matched(at, step, half):
        by = step + 1
        shift = by if half == 1 else clusters - by
        index = (at * ROUNDS + step) * 2 + half
        rows = pl.ds((1 - half) * BLOCK, BLOCK)
        return remote(
            near.at[at, rows],
            far.at[at, step, half],
            g_send.at[index],
            g_recv.at[index],
            (lax.rem(row + shift, clusters), me),
        )

    def meta_move(offset):
        peer = after(offset)
        return remote(
            meta_ref, meta_in.at[me], m_send.at[offset], m_recv.at[offset], (row, peer)
        )

    def all_matched(kinds):
        return [matched(at, step, half) for at in kinds for step in range(ROUNDS) for half in range(2)]

    metas = [meta_move(offset) for offset in range(1, team)]
    kv_moves = [across(kv_out, kv_in, kv_send, kv_recv, offset) for offset in range(1, team)]
    qg_moves = [across(qg_out, qg_in, qg_send, qg_recv, offset) for offset in range(1, team)]
    first = all_matched((k_at, v_at))
    second = all_matched((q_at, g_at))
    for copy in metas + first + kv_moves:
        copy.start()
    pack(qg_out, q_at, g_at)
    for copy in qg_moves:
        copy.start()
    kv_in[me] = kv_out[me]
    qg_in[me] = qg_out[me]
    meta_in[me] = meta_ref[...]
    zw_all[blocks * TMAX] = jnp.zeros((BLOCK, 2 * BLOCK), BF16)
    for copy in metas:
        copy.wait()
    to_scalar = pltpu.make_async_copy(meta_in, meta_s, meta_sem)
    to_scalar.start()
    to_scalar.wait()
    for copy in kv_moves:
        copy.wait()

    def turn(unit, carry):
        for half in range(2):
            kvt[2 * unit + half] = kv_in[unit, half].astype(F32).T.astype(BF16)
        return carry

    lax.fori_loop(0, team, turn, 0)

    lane = lax.broadcasted_iota(jnp.int32, (BLOCK, BLOCK), 1) < HEAD_DIM

    def attend_local(unit, half):
        block = 2 * unit + half
        qg = qg_in[unit, half].astype(F32)
        split = jnp.concatenate([jnp.where(lane, qg * SCALE, 0.0), jnp.where(lane, 0.0, qg)], 0)
        split = split.astype(BF16)
        qg2[block] = split
        live = meta_s[unit, half, TMAX]
        s_loc = []
        top = None
        for slot in range(TMAX):
            source = meta_s[unit, half, slot]
            both = dot_last(kv_in[source // 2, source % 2], split)
            scores = both[:, :BLOCK] + jnp.where(slot < live, 0.0, NEG_BIG)
            s_loc.append(scores)
            d_all[block * TMAX + slot] = both[:, BLOCK:]
            most = jnp.max(scores, 0, keepdims=True)
            top = most if top is None else jnp.maximum(top, most)
        total, weighted = None, None
        for slot in range(TMAX):
            e = jnp.exp(s_loc[slot] - top)
            e_all[block * TMAX + slot] = e
            part = jnp.sum(e, 0, keepdims=True)
            other = jnp.sum(e * d_all[block * TMAX + slot], 0, keepdims=True)
            total = part if total is None else total + part
            weighted = other if weighted is None else weighted + other
        stats[block] = jnp.concatenate(
            [top, total, weighted, jnp.zeros((5, BLOCK), F32)], 0
        )

    for half in range(2):
        attend_local(me, half)

    for copy in first:
        copy.wait()
    for copy in second:
        copy.start()
    marks = [head_marks(8 * HEADS, slot, width) for slot in range(2 * ROUNDS)]
    for half in range(2):
        rows = slice(half * BLOCK, (half + 1) * BLOCK)
        total = None
        for step in range(ROUNDS):
            pick = pick_rows(partner_ref[step : step + 1, rows])
            for at, (kind, own) in enumerate(((k_at, q_at), (v_at, g_at))):
                taken = dot(pick, far[kind, step, half])
                picked[at, step, rows] = taken.astype(BF16)
                product = near[own, rows].astype(F32) * taken
                high = product.astype(BF16)
                low = (product - high.astype(F32)).astype(BF16)
                mark = marks[at * ROUNDS + step]
                part = dot_last(mark, high) + dot_last(mark, low)
                total = part if total is None else total + part
        pair_out[:, half] = total.reshape(HEADS, 8, BLOCK)
    pairs = [across(pair_out, pair_in, p_send, p_recv, offset) for offset in range(1, team)]
    for copy in pairs:
        copy.start()
    pair_in[me] = pair_out[me]

    def attend_pair(unit, half):
        block = 2 * unit + half
        ids = [meta_s[unit, half, slot] for slot in range(TMAX)]
        held = stats[block]
        top_loc, total_loc, dot_loc = held[0:1], held[1:2], held[2:3]
        pair = pair_in[unit, half]
        s_pair = [pair[r : r + 1] * SCALE for r in range(ROUNDS)]
        d_pair = [pair[ROUNDS + r : ROUNDS + r + 1] for r in range(ROUNDS)]
        top = functools.reduce(jnp.maximum, s_pair, top_loc)
        shrink = jnp.exp(top_loc - top)
        e_pair = [jnp.exp(s - top) for s in s_pair]
        inverse = 1.0 / functools.reduce(jnp.add, e_pair, total_loc * shrink)
        factor = shrink * inverse
        p_pair = [e * inverse for e in e_pair]
        delta = functools.reduce(
            jnp.add, [p * d for p, d in zip(p_pair, d_pair)], dot_loc * factor
        )
        w_pair = [p.astype(BF16).astype(F32) for p in p_pair]
        z_pair = [(p * (d - delta)).astype(BF16).astype(F32) for p, d in zip(p_pair, d_pair)]
        pw_out[unit, half] = jnp.concatenate(
            w_pair + z_pair + [jnp.zeros((8 - 2 * ROUNDS, BLOCK), F32)], 0
        )
        back = None
        for slot in range(TMAX):
            p = e_all[block * TMAX + slot] * factor
            z = (p * (d_all[block * TMAX + slot] - delta)).astype(BF16)
            zw = jnp.concatenate([z, p.astype(BF16)], 1)
            zw_all[block * TMAX + slot] = zw
            part = dot(kvt[ids[slot]], zw)
            back = part if back is None else back + part
        turned = jnp.concatenate([back[:HEAD_DIM, :BLOCK] * SCALE, back[HEAD_DIM:, BLOCK:]], 0)
        oq_out[unit, half] = turned.T.astype(BF16)

    def attend_unit(offset, carry):
        unit = before(offset)

        @pl.when(offset > 0)
        def _():
            across(qg_out, qg_in, qg_send, qg_recv, offset).wait()
            for half in range(2):
                attend_local(unit, half)
            across(pair_out, pair_in, p_send, p_recv, offset).wait()

        for half in range(2):
            attend_pair(unit, half)

        @pl.when(offset > 0)
        def _():
            back_to(pw_out, pw_in, w_send, w_recv, offset).start()
            back_to(oq_out, oq_in, o_send, o_recv, offset).start()

        return carry

    lax.fori_loop(0, team, attend_unit, 0)
    pw_in[me] = pw_out[me]
    oq_in[me] = oq_out[me]

    def key_grads(at, carry):
        offset = team - 1 - at
        unit = before(offset)
        for half in range(2):
            block = 2 * unit + half
            live = meta_s[unit, half, TMAX]
            total = None
            for slot in range(TMAX):
                other = meta_s[unit, half, slot]
                place = jnp.int32(0)
                for there in range(1, TMAX):
                    same = meta_s[other // 2, other % 2, there] == block
                    place = jnp.where(same, jnp.int32(there), place)
                index = jnp.where(slot < live, other * TMAX + place, blocks * TMAX)
                part = dot(zw_all[index], qg2[other])
                total = part if total is None else total + part
            dkv_out[unit, half] = total.astype(BF16)

        @pl.when(offset > 0)
        def _():
            back_to(dkv_out, dkv_in, d_send, d_recv, offset).start()

        return carry

    lax.fori_loop(0, team, key_grads, 0)
    dkv_in[me] = dkv_out[me]

    for offset in range(1, team):
        back_to(pw_out, pw_in, w_send, w_recv, offset).wait()
    forwards = []
    for step in range(ROUNDS):
        by = step + 1
        for half in range(2):
            shift = by if half == 0 else clusters - by
            index = step * 2 + half
            copy = remote(
                pw_in.at[:, half],
                pw_far.at[step, 1 - half],
                f_send.at[index],
                f_recv.at[index],
                (lax.rem(row + shift, clusters), me),
            )
            copy.start()
            forwards.append(copy)
    marks = [head_marks(BLOCK, slot, width) for slot in range(2 * ROUNDS)]

    def by_node(flat):
        flat = flat.reshape(8 * HEADS, BLOCK)
        flat = jnp.concatenate([flat, jnp.zeros((BLOCK - 8 * HEADS, BLOCK), F32)], 0)
        return flat.T.astype(BF16)

    def heads_of(buf, half, left):
        parts = [buf[head, half][:, left : left + HEAD_DIM] for head in range(team)]
        return jnp.concatenate(parts, 1).astype(F32)

    for offset in range(1, team):
        back_to(oq_out, oq_in, o_send, o_recv, offset).wait()
    for half in range(2):
        rows = slice(half * BLOCK, (half + 1) * BLOCK)
        turned = by_node(pw_in[:, half])
        attended = heads_of(oq_in, half, HEAD_DIM)
        query_grad = heads_of(oq_in, half, 0)
        for step in range(ROUNDS):
            w = dot(turned, marks[step])
            z = dot(turned, marks[ROUNDS + step]) * SCALE
            attended += w * picked[1, step, rows].astype(F32)
            query_grad += z * picked[0, step, rows].astype(F32)
        out_ref[rows] = attended.astype(BF16)
        dq_ref[rows] = query_grad.astype(BF16)

    for copy in second + forwards:
        copy.wait()
    backs = []
    for half in range(2):
        rows = slice(half * BLOCK, (half + 1) * BLOCK)
        back_key, back_value = None, None
        for step in range(ROUNDS):
            turned = by_node(pw_far[step, half])
            pick = pick_rows(partner_ref[step : step + 1, rows])
            w = dot(turned, marks[step])
            z = dot(turned, marks[ROUNDS + step]) * SCALE
            term_key = (z * far[q_at, step, half].astype(F32)).astype(BF16)
            term_value = (w * far[g_at, step, half].astype(F32)).astype(BF16)
            part_key, part_value = dot(pick, term_key), dot(pick, term_value)
            back_key = part_key if back_key is None else back_key + part_key
            back_value = part_value if back_value is None else back_value + part_value
        backs.append((back_key, back_value))
    for offset in range(1, team):
        back_to(dkv_out, dkv_in, d_send, d_recv, offset).wait()
    for half in range(2):
        rows = slice(half * BLOCK, (half + 1) * BLOCK)
        dk_ref[rows] = (heads_of(dkv_in, half, 0) + backs[half][0]).astype(BF16)
        dv_ref[rows] = (heads_of(dkv_in, half, HEAD_DIM) + backs[half][1]).astype(BF16)


def write_kernel(*refs):
    held, in_sems, out_sems = refs[8:]
    copies = [pltpu.make_async_copy(refs[at], held.at[at], in_sems.at[at]) for at in range(4)]
    writes = [pltpu.make_async_copy(held.at[at], refs[4 + at], out_sems.at[at]) for at in range(4)]
    for copy in copies:
        copy.start()
    for copy, write in zip(copies, writes):
        copy.wait()
        write.start()
    for write in writes:
        write.wait()


def shards(clusters, team, query, key, value, out_grad, partner, tiles, tile_count):
    nodes, width = query.shape
    shape = jax.ShapeDtypeStruct
    whole = pl.BlockSpec(memory_space=VMEM)
    scalar = pl.BlockSpec(memory_space=pltpu.SMEM)
    anywhere = pl.BlockSpec(memory_space=pl.ANY)
    dma = pltpu.SemaphoreType.DMA
    blocks = 2 * team
    big = VMEM((team, 2, BLOCK, BLOCK), BF16)
    few = VMEM((team, 2, 8, BLOCK), F32)
    metas = (team, 8, 128)
    results = pl.pallas_call(
        functools.partial(fused_kernel, clusters, team),
        out_shape=(shape((nodes, width), BF16),) * 4,
        in_specs=[anywhere] * 5 + [scalar] * 2,
        out_specs=(whole,) * 4,
        scratch_shapes=[
            VMEM((4, nodes, width), BF16),
            VMEM((4, ROUNDS, 2, BLOCK, width), BF16),
            VMEM((ROUNDS, nodes), jnp.int32),
            VMEM((8, 128), jnp.int32),
            big,
            big,
            big,
            big,
            few,
            few,
            VMEM(metas, jnp.int32),
            pltpu.SMEM(metas, jnp.int32),
            VMEM((2, ROUNDS, nodes, width), BF16),
            VMEM((blocks, 2 * BLOCK, BLOCK), BF16),
            VMEM((blocks, BLOCK, BLOCK), BF16),
            VMEM((blocks * TMAX + 1, BLOCK, 2 * BLOCK), BF16),
            VMEM((blocks * TMAX, BLOCK, BLOCK), F32),
            VMEM((blocks * TMAX, BLOCK, BLOCK), F32),
            VMEM((blocks, 8, BLOCK), F32),
            big,
            big,
            big,
            big,
            few,
            few,
            VMEM((ROUNDS, 2, team, 8, BLOCK), F32),
            dma((5,)),
            dma,
        ]
        + [dma((team,))] * 14
        + [dma((8 * ROUNDS,))] * 2
        + [dma((2 * ROUNDS,))] * 2,
        compiler_params=pltpu.CompilerParams(
            collective_id=0, has_side_effects=True, vmem_limit_bytes=LIMIT
        ),
    )(query, key, value, out_grad, partner, tiles, tile_count)
    return pl.pallas_call(
        write_kernel,
        out_shape=(shape((nodes, width), BF16),) * 4,
        in_specs=[anywhere] * 4,
        out_specs=(anywhere,) * 4,
        scratch_shapes=[VMEM((4, nodes, width), BF16), dma((4,)), dma((4,))],
    )(*results)


def solution(mesh):
    rows = P(("grp", "blk"), None)
    in_specs = (rows, rows, rows, rows, P(None, ("grp", "blk")), rows, P(("grp", "blk")))
    return jax.shard_map(
        functools.partial(shards, mesh.shape["grp"], mesh.shape["blk"]),
        mesh=mesh,
        in_specs=in_specs,
        out_specs=(rows,) * 4,
        check_vma=False,
    )
```
